32 devices in a mesh: seq: 32 (over z, y, x, core), tp: 1.
Axes of the slice: x: 2, y: 2, z: 4, core: 2. Of those that a mesh axis runs over, the one named last changes fastest.
Arguments:
- hidden_in: bfloat16 [4, 2048, 4096], P(None, 'seq'), may hold values from -6 to 6
- ln_gain: float32 [4096], replicated, may hold values from 0.1 to 1.9
- ln_bias: float32 [4096], replicated, may hold values from -3 to 3
- w_qkv: bfloat16 [3, 4096, 4096], P(None, 'seq', 'tp'), may hold values from -0.09375 to 0.09375
- w_out: bfloat16 [4096, 4096], P('tp', 'seq'), may hold values from -1.5 to 1.5
- cache_kv: bfloat16 [4, 512, 2, 4096], P(None, 'seq', None, 'tp'), may hold values from -500 to 500
- cache_len: int32 [4], replicated, may hold values from 128 to 512, as said below
- owner: int32 [8192, 1], P('seq'), may hold values from 0 to 31; in each aligned block of 256 rows (0 to 255, 256 to 511, ...) at most 8 rows name the same one
Outputs:
- attn_out: bfloat16 [4, 2048, 4096], P(None, 'seq', 'tp')
- appended: bfloat16 [8192, 2, 4096], P('seq', None, 'tp')
The draws below stay inside these ranges and needn't reach their ends.
Inputs may be any that keep to these rules, and one draw needn't show every extreme that they name: `cache_len`: at least 128; one request's cache holds exactly 512 positions. Among the 256 tokens of one device no owner is named more than 8 times.
All inputs are finite; a program needn't handle non-finite values.
Results may differ from the reference program's by a relative error of at most 0.013.
The reference program's roundings to bfloat16 on the way count: a program that leaves them out, or rounds other values in their place, can miss the bound.
Values may be sent and summed in bfloat16 or wider, within the bound.
No kernel may reach another device: no remote copies, remote signals or barrier semaphores. Data moves between devices by JAX's collectives and lax.ppermute only.
A program may use at most 512 MiB of HBM per device.

```python
import math
import jax
import jax.numpy as jnp
import numpy as np
from jax import lax

D = 4096
HEADS = 16
HD = 256
ROT = 64
REQ = 4
SLOTS = 8
TOK_DEV = 256
TOKENS = 8192
NEW_LEN = 2048
CACHE = 512
N_SEQ = 32
N_TP = 1


def draw_cache_kv(key, part):
    columns = HEADS * HD
    shape_all = (REQ, CACHE, 2, columns)
    base = jnp.clip(jax.random.normal(jax.random.fold_in(key, 11), shape_all, jnp.float32), -6.0, 6.0)
    return base.astype(jnp.bfloat16)


def draw_cache_len(key, part):
    lengths = jax.random.randint(jax.random.fold_in(key, 21), (REQ,), CACHE // 4, CACHE + 1)
    chosen = jax.random.randint(jax.random.fold_in(key, 22), (), 0, REQ)
    return jnp.where(jnp.arange(REQ) == chosen, CACHE, lengths).astype(jnp.int32)


def steps_of(stream_key, dims, split, low, largest):
    loudness, own = 1.0, jax.random.fold_in(stream_key, 6)
    for dim, parts in split:
        draws = jnp.exp(jax.random.uniform(jax.random.fold_in(own, dim), (parts,), jnp.float32, low / len(split), largest / len(split)))
        loudness = loudness * jnp.repeat(draws, dims[dim] // parts).reshape([-1 if axis == dim else 1 for axis in range(len(dims))])
    return loudness


def assign_block(key, own, number, rows, amount, top, bound, lean):
    ranking = jax.random.permutation(key, amount)
    packed, usual = shares(amount, rows * top, bound, lean, True), shares(amount, rows * top, bound, lean, False)
    places = jnp.arange(amount)

    def named(sizes, rotation):
        used = int((sizes > 0).sum())
        fixed = max(1, used // 4)
        moved = fixed + (places - fixed + rotation * (used - fixed)) % max(1, amount - fixed)
        return jnp.zeros((amount,), jnp.int32).at[ranking[jnp.where(places < fixed, places, moved)]].set(jnp.asarray(sizes, jnp.int32))

    sizes = jnp.where(number % 4 == 0, named(packed, number // 4), named(usual, number - number // 4 - 1))
    mixed = jax.random.permutation(jax.random.fold_in(own, 3), amount)
    giver, taker = mixed[0:amount // 2 * 2:2], mixed[1:amount // 2 * 2:2]
    room = jnp.minimum(sizes[giver] - 1, bound - sizes[taker]) // 2
    room = jnp.where((giver == ranking[0]) | (taker == ranking[0]) | (sizes[taker] == 0), 0, jnp.maximum(room, 0))
    moved = jax.random.randint(jax.random.fold_in(own, 4), (amount // 2,), 0, 1 << 20) % (room + 1)
    sizes = sizes.at[giver].add(-moved).at[taker].add(moved)
    labels = jnp.searchsorted(jnp.cumsum(sizes), jnp.arange(rows * top), side="right").astype(jnp.int32)
    grid = labels.reshape(top, rows).T
    grid = grid[jax.random.permutation(jax.random.fold_in(own, 1), rows)]
    rotation = jax.random.randint(jax.random.fold_in(own, 2), (rows, 1), 0, top)
    return jnp.take_along_axis(grid, (jnp.arange(top)[None, :] + rotation) % top, axis=1)


def shares(amount, total, most, skew, full):
    portions = [(1 << 20) // math.isqrt(standing ** skew) + 1 for standing in range(1, amount + 1)]
    largest = most if full else min(most, max(-(-total // amount), total * portions[0] // sum(portions)))
    least = 1 if total - largest >= amount - 1 else 0
    given, rest = [largest] + [least] * (amount - 1), total - largest - least * (amount - 1)
    while rest > 0:
        movable = [i for i in range(1, amount) if given[i] < largest] or [i for i in range(1, amount) if given[i] < most]
        pool, remaining = sum([portions[i] for i in movable]), rest
        for i in movable:
            extra = min(most - given[i], max(1, remaining * portions[i] // pool), rest)
            given[i] = given[i] + extra
            rest = rest - extra
    return np.array(given)


def gaussian(own_key, extent, scale, bound, split=(), dtype=jnp.bfloat16):
    array = scale * jax.random.normal(own_key, extent, jnp.float32)
    if split:
        array = array * steps_of(own_key, extent, split, -0.22, 0.18)
    return jnp.clip(array, -bound, bound).astype(dtype)


def setup_inputs(seed: int = 0) -> dict:
    arg_keys = jax.random.split(jax.random.key(seed), 9)
    hidden_in = gaussian(arg_keys[0], (REQ, NEW_LEN, D), 1.0, 6.0, ((1, 32),))
    ln_gain = jnp.clip(1.0 + 0.18 * jax.random.normal(arg_keys[1], (D,), jnp.float32), 0.1, 1.9)
    ln_bias = gaussian(arg_keys[2], (D,), 0.5, 3.0, (), jnp.float32)
    w_qkv = gaussian(arg_keys[3], (3, D, HEADS * HD), D ** -0.5, 0.09375, ((1, 32),))
    w_out = gaussian(arg_keys[4], (HEADS * HD, D), HEADS ** -0.5, 1.5, ((1, 32),))
    cache_kv = draw_cache_kv(jax.random.fold_in(arg_keys[8], 71), 0)
    cache_len = draw_cache_len(jax.random.fold_in(arg_keys[8], 71), 0)
    owner_keys = jax.random.split(jax.random.fold_in(arg_keys[7], 1), TOKENS // TOK_DEV)
    owner_turns = jax.random.permutation(jax.random.fold_in(arg_keys[7], 3), TOKENS // TOK_DEV)
    owner = jax.vmap(lambda own, number: assign_block(jax.random.fold_in(arg_keys[7], 2), own, number, TOK_DEV, N_SEQ, 1, SLOTS, 2))(owner_keys, owner_turns).reshape((TOKENS, 1))
    return {"hidden_in": hidden_in, "ln_gain": ln_gain, "ln_bias": ln_bias, "w_qkv": w_qkv, "w_out": w_out, "cache_kv": cache_kv, "cache_len": cache_len, "owner": owner}


EPSILON = 1e-05
BASE_FREQ = 10000.0
MASKED = -1e+30

def layer_norm(values_in, gain, shift):
    wide = values_in.astype(jnp.float32)
    center = lax.optimization_barrier(jnp.mean(wide, axis=-1, keepdims=True))
    spread = wide - center
    variance = lax.optimization_barrier(jnp.mean(spread * spread, axis=-1, keepdims=True))
    return (spread * lax.rsqrt(variance + EPSILON) * gain + shift).astype(jnp.bfloat16)

def rotate(heads_in, positions):
    pair_index = jnp.arange(ROT // 2).astype(jnp.float32)
    inverse = jnp.power(BASE_FREQ, -2.0 * pair_index / ROT)
    angles = positions.astype(jnp.float32)[:, None] * inverse[None, :]
    cosine = jnp.cos(angles)[:, None, :]
    sine = jnp.sin(angles)[:, None, :]
    leading = heads_in.shape[:-1]
    paired = heads_in[..., :ROT].reshape(leading + (ROT // 2, 2))
    even = paired[..., 0]
    odd = paired[..., 1]
    turned = jnp.stack([even * cosine - odd * sine, odd * cosine + even * sine], axis=-1).reshape(leading + (ROT,))
    return jnp.concatenate([turned, heads_in[..., ROT:]], axis=-1)

def reference(hidden_in, ln_gain, ln_bias, w_qkv, w_out, cache_kv, cache_len, owner):
    normed = layer_norm(hidden_in.reshape(TOKENS, D), ln_gain, ln_bias)
    token_ids = jnp.arange(TOKENS).astype(jnp.int32)
    request = token_ids // NEW_LEN
    positions = cache_len[request] + token_ids % NEW_LEN
    shape_heads = (TOKENS, HEADS, HD)
    query = rotate(jnp.dot(normed, w_qkv[0], preferred_element_type=jnp.float32).reshape(shape_heads), positions).astype(jnp.bfloat16)
    keys_new = rotate(jnp.dot(normed, w_qkv[1], preferred_element_type=jnp.float32).reshape(shape_heads), positions).astype(jnp.bfloat16)
    values_new = jnp.dot(normed, w_qkv[2], preferred_element_type=jnp.float32).reshape(shape_heads).astype(jnp.bfloat16)
    cache_all = cache_kv.reshape(REQ, CACHE, 2, HEADS, HD)
    scale_factor = 1.0 / math.sqrt(HD)

    def one_request(which):
        start = which * NEW_LEN
        query_rows = lax.dynamic_slice_in_dim(query, start, NEW_LEN, 0).astype(jnp.float32)
        key_fresh = lax.dynamic_slice_in_dim(keys_new, start, NEW_LEN, 0)
        value_fresh = lax.dynamic_slice_in_dim(values_new, start, NEW_LEN, 0)
        cached = lax.dynamic_index_in_dim(cache_all, which, 0, keepdims=False)
        key_rows = jnp.concatenate([cached[:, 0], key_fresh], axis=0).astype(jnp.float32)
        value_rows = jnp.concatenate([cached[:, 1], value_fresh], axis=0).astype(jnp.float32)
        length = lax.dynamic_index_in_dim(cache_len, which, 0, keepdims=False)
        query_pos = length + jnp.arange(NEW_LEN).astype(jnp.int32)
        key_pos = jnp.concatenate([jnp.arange(CACHE).astype(jnp.int32), query_pos])
        usable = jnp.concatenate([jnp.arange(CACHE).astype(jnp.int32) < length, jnp.ones((NEW_LEN,), jnp.bool_)])
        allowed = usable[None, :] & (key_pos[None, :] <= query_pos[:, None])
        scores = jnp.einsum('qhd,khd->hqk', query_rows, key_rows) * scale_factor
        scores = jnp.where(allowed[None], scores, MASKED)
        highest = lax.optimization_barrier(jnp.max(scores, axis=-1, keepdims=True))
        weights = jnp.where(allowed[None], jnp.exp(scores - highest), 0.0)
        weight_sum = lax.optimization_barrier(jnp.sum(weights, axis=-1))
        rounded = lax.optimization_barrier(weights.astype(jnp.bfloat16)).astype(jnp.float32)
        mixed = jnp.einsum('hqk,khd->qhd', rounded, value_rows)
        return (mixed / jnp.transpose(weight_sum)[:, :, None]).astype(jnp.bfloat16)
    attended = lax.map(one_request, jnp.arange(REQ).astype(jnp.int32)).reshape(TOKENS, HEADS * HD)
    group_cols = HEADS * HD // N_TP

    def add_group(total, which):
        piece = lax.dynamic_slice_in_dim(attended, which * group_cols, group_cols, 1)
        weight_rows = lax.dynamic_slice_in_dim(w_out, which * group_cols, group_cols, 0)
        term = lax.optimization_barrier(jnp.dot(piece, weight_rows, preferred_element_type=jnp.float32).astype(jnp.bfloat16))
        return (total + term.astype(jnp.float32), None)
    summed, unused = lax.scan(add_group, jnp.zeros((TOKENS, D), jnp.float32), jnp.arange(N_TP).astype(jnp.int32))
    attn_out = summed.astype(jnp.bfloat16).reshape(REQ, NEW_LEN, D)
    new_dev = TOK_DEV // REQ
    fresh = jnp.stack([keys_new.reshape(TOKENS, HEADS * HD), values_new.reshape(TOKENS, HEADS * HD)], axis=1)
    fresh = fresh.reshape(REQ, N_SEQ, new_dev, 2, HEADS * HD).transpose(1, 0, 2, 3, 4).reshape(TOKENS, 2, HEADS * HD)
    owners = owner[:, 0]
    grouped = owners.reshape(N_SEQ, TOK_DEV)
    marks = (grouped[:, :, None] == jnp.arange(N_SEQ).astype(jnp.int32)[None, None, :]).astype(jnp.int32)
    earlier = jnp.cumsum(marks, axis=1) - marks
    slot_ids = lax.optimization_barrier(jnp.sum(earlier * marks, axis=-1)).reshape(TOKENS)
    sender = token_ids // TOK_DEV
    target_rows = owners * (N_SEQ * SLOTS) + sender * SLOTS + slot_ids
    appended = jnp.zeros((N_SEQ * N_SEQ * SLOTS, 2, HEADS * HD), jnp.bfloat16).at[target_rows].set(fresh)
    return (attn_out, appended)
```

```python
import functools
import math

import jax
import jax.numpy as jnp
from jax import lax
from jax.experimental import pallas as pl
from jax.experimental.pallas import tpu as pltpu
from jax.sharding import Mesh
from jax.sharding import PartitionSpec as P

HD = 256
ROT = 64
REQ = 4
SLOTS = 8
CORES = 2

EPSILON = 1e-05
BASE_FREQ = 10000.0
MASKED = -1e30
LANES = 128


def layer_norm(values_in, gain, shift):
    wide = values_in.astype(jnp.float32)
    center = jnp.mean(wide, axis=-1, keepdims=True)
    spread = wide - center
    variance = jnp.mean(spread * spread, axis=-1, keepdims=True)
    return (spread * lax.rsqrt(variance + EPSILON) * gain + shift).astype(jnp.bfloat16)


def rotate(heads_in, positions):
    pair_index = jnp.arange(ROT // 2).astype(jnp.float32)
    inverse = jnp.power(BASE_FREQ, -2.0 * pair_index / ROT)
    angles = positions.astype(jnp.float32)[:, None] * inverse[None, :]
    cosine = jnp.cos(angles)[:, None, :]
    sine = jnp.sin(angles)[:, None, :]
    leading = heads_in.shape[:-1]
    paired = heads_in[..., :ROT].reshape(leading + (ROT // 2, 2))
    even = paired[..., 0]
    odd = paired[..., 1]
    turned = jnp.stack([even * cosine - odd * sine, odd * cosine + even * sine], axis=-1).reshape(
        leading + (ROT,)
    )
    return jnp.concatenate([turned, heads_in[..., ROT:]], axis=-1)


def rotary_tables(positions):
    lane = jnp.arange(LANES)
    pair_index = (lane // 2).astype(jnp.float32)
    inverse = jnp.power(BASE_FREQ, -2.0 * pair_index / ROT)
    angles = positions.astype(jnp.float32)[:, None] * inverse[None, :]
    turned = lane < ROT
    cosine = jnp.where(turned, jnp.cos(angles), 1.0)
    sine = jnp.where(turned, jnp.where(lane % 2 == 0, -1.0, 1.0) * jnp.sin(angles), 0.0)
    return cosine, sine


def project_kernel(
    place, x_ref, w0, w1, w2, w3, cos_ref, sin_ref, q_ref, k_ref, v_ref, send_ref, held, sem
):
    zs, rows_each = held.shape[1] // (REQ * CORES * w0.shape[2]), w0.shape[2]
    width = held.shape[2]
    here = place[0]

    @pl.when(pl.program_id(0) == 0)
    def _():
        copies = []
        for away, source in enumerate((w0, w1, w2, w3)):
            chip = here ^ away
            for z in range(zs):
                for c in range(CORES):
                    row = pl.multiple_of(((z * REQ + chip) * CORES + c) * rows_each, rows_each)
                    for which in range(3):
                        copies.append(
                            pltpu.make_async_copy(
                                source.at[z * CORES + c, which],
                                held.at[which, pl.ds(row, rows_each)],
                                sem.at[len(copies)],
                            )
                        )
        for copy in copies:
            copy.start()
        for copy in copies:
            copy.wait()

    each = x_ref.shape[2]
    rows = x_ref[...].reshape(CORES * REQ * each, x_ref.shape[3])
    lane = lax.broadcasted_iota(jnp.int32, (each, LANES), 1)
    even = lane % 2 == 0
    for which in range(3):
        out = jnp.dot(rows, held[which], preferred_element_type=jnp.float32)
        for c in range(CORES):
            for r in range(REQ):
                start = (c * REQ + r) * each
                part = out[start : start + each]
                if which < 2:
                    cosine, sine = cos_ref[0, r, c], sin_ref[0, r, c]
                    pieces = []
                    for head in range(width // HD):
                        low = part[:, head * HD : head * HD + LANES]
                        other = jnp.where(
                            even, pltpu.roll(low, LANES - 1, 1), pltpu.roll(low, 1, 1)
                        )
                        pieces.append(low * cosine + other * sine)
                        pieces.append(part[:, head * HD + LANES : (head + 1) * HD])
                    part = jnp.concatenate(pieces, axis=1)
                part = part.astype(jnp.bfloat16)
                if which == 0:
                    q_ref[0, r, c] = part
                elif which == 1:
                    k_ref[0, r, c] = part
                    send_ref[r, 0, c, :, :width] = part
                else:
                    v_ref[0, r, c] = part
                    send_ref[r, 0, c, :, width:] = part


def project(x_all, weights, cosine, sine, chip):
    zs = x_all.shape[0] // CORES
    each, depth = x_all.shape[2], x_all.shape[3]
    rows_each, width = weights[0].shape[2], weights[0].shape[3]
    table = pl.BlockSpec((1, REQ, CORES, each, LANES), lambda z, s: (z, 0, 0, 0, 0))
    token = pl.BlockSpec((1, REQ, CORES, each, width), lambda z, s: (z, 0, 0, 0, 0))
    by_token = jax.ShapeDtypeStruct((zs, REQ, CORES, each, width), jnp.bfloat16)
    return pl.pallas_call(
        project_kernel,
        grid_spec=pltpu.PrefetchScalarGridSpec(
            num_scalar_prefetch=1,
            grid=(zs,),
            in_specs=[pl.BlockSpec((CORES, REQ, each, depth), lambda z, s: (z, 0, 0, 0))]
            + [pl.BlockSpec(memory_space=pl.ANY)] * 4
            + [table, table],
            out_specs=[
                token,
                token,
                token,
                pl.BlockSpec((REQ, 1, CORES, each, 2 * width), lambda z, s: (0, z, 0, 0, 0)),
            ],
            scratch_shapes=[
                pltpu.VMEM((3, depth, width), jnp.bfloat16),
                pltpu.SemaphoreType.DMA((4 * zs * CORES * 3,)),
            ],
        ),
        out_shape=[
            by_token,
            by_token,
            by_token,
            jax.ShapeDtypeStruct((REQ, zs, CORES, each, 2 * width), jnp.bfloat16),
        ],
        compiler_params=pltpu.CompilerParams(
            vmem_limit_bytes=56 * 2**20, dimension_semantics=("arbitrary",)
        ),
        cost_estimate=pl.CostEstimate(
            flops=2 * zs * CORES * REQ * each * depth * 3 * width,
            bytes_accessed=2 * (x_all.size + 3 * depth * width * 2),
            transcendentals=0,
        ),
    )(jnp.reshape(chip, (1,)).astype(jnp.int32), x_all, *weights, cosine, sine)


def attend_kernel(length, q_ref, k_ref, v_ref, kc_ref, vc_ref, o_ref, *, blocks):
    step = pl.program_id(1)
    size = q_ref.shape[0]
    factor = math.log2(math.e) / math.sqrt(HD)
    contract = (((1,), (1,)), ((), ()))
    slots = kc_ref.shape[0] * kc_ref.shape[1]

    for index in range(blocks):

        @pl.when(step == index)
        def _(index=index):
            query = q_ref[...]
            k_old = kc_ref[...].reshape(slots, HD)
            v_old = vc_ref[...].reshape(slots, HD)
            old = lax.dot_general(query, k_old, contract, preferred_element_type=jnp.float32)
            slot = lax.broadcasted_iota(jnp.int32, old.shape, 1)
            old = jnp.where(slot < length[0], old, MASKED)
            parts = [(old, v_old)]
            if index:
                span = index * size
                parts.append(
                    (
                        lax.dot_general(
                            query, k_ref[:span], contract, preferred_element_type=jnp.float32
                        ),
                        v_ref[:span],
                    )
                )
            own = lax.dot_general(
                query,
                k_ref[index * size : (index + 1) * size],
                contract,
                preferred_element_type=jnp.float32,
            )
            row = lax.broadcasted_iota(jnp.int32, own.shape, 0)
            column = lax.broadcasted_iota(jnp.int32, own.shape, 1)
            own = jnp.where(column <= row, own, MASKED)
            parts.append((own, v_ref[index * size : (index + 1) * size]))
            highest = functools.reduce(
                jnp.maximum, [jnp.max(s, axis=1, keepdims=True) for s, _ in parts]
            )
            total, mixed = 0.0, 0.0
            for scores, values in parts:
                weights = jnp.exp2((scores - highest) * factor)
                total = total + jnp.sum(weights, axis=1, keepdims=True)
                mixed = mixed + jnp.dot(
                    weights.astype(jnp.bfloat16), values, preferred_element_type=jnp.float32
                )
            o_ref[...] = (mixed / total).astype(jnp.bfloat16)


def attend(query, keys, values, cached, length):
    count, width = query.shape
    heads, size = width // HD, min(256, count)
    blocks = count // size
    sources, _, each, _ = cached.shape

    def old(which):
        return pl.BlockSpec((sources, None, each, HD), lambda h, i, s: (0, which, 0, h))

    return pl.pallas_call(
        functools.partial(attend_kernel, blocks=blocks),
        grid_spec=pltpu.PrefetchScalarGridSpec(
            num_scalar_prefetch=1,
            grid=(heads, blocks),
            in_specs=[
                pl.BlockSpec((size, HD), lambda h, i, s: (i, h)),
                pl.BlockSpec((count, HD), lambda h, i, s: (0, h)),
                pl.BlockSpec((count, HD), lambda h, i, s: (0, h)),
                old(0),
                old(1),
            ],
            out_specs=pl.BlockSpec((size, HD), lambda h, i, s: (i, h)),
        ),
        out_shape=jax.ShapeDtypeStruct((count, width), jnp.bfloat16),
        compiler_params=pltpu.CompilerParams(
            vmem_limit_bytes=48 * 2**20, dimension_semantics=("arbitrary", "arbitrary")
        ),
        cost_estimate=pl.CostEstimate(
            flops=4 * count * (count // 2 + sources * each) * width,
            bytes_accessed=2 * 4 * count * width,
            transcendentals=count * (count // 2 + sources * each) * heads,
        ),
    )(jnp.reshape(length, (1,)), query, keys, values, cached, cached)


def slots_of(owners, count):
    marks = (owners[:, None] == jnp.arange(count)[None, :]).astype(jnp.int32)
    earlier = jnp.cumsum(marks, axis=0) - marks
    return owners * SLOTS + jnp.sum(earlier * marks, axis=1)


def by_heads(hidden_in, ln_gain, ln_bias, w_qkv, w_out, cache_kv, cache_len, owner):
    zs, seq_count = lax.axis_size("z"), lax.axis_size("z") * REQ * CORES
    groups = zs * CORES
    chip = lax.axis_index("r")
    seq = ("z", "r", "c")
    new_dev, depth = hidden_in.shape[1], hidden_in.shape[2]
    width = w_qkv.shape[2]
    cols = width // groups

    w_cut = w_qkv.reshape(3, w_qkv.shape[1], groups, cols).transpose(2, 0, 1, 3)
    w_own = lax.all_to_all(w_cut, ("z", "c"), split_axis=0, concat_axis=0, tiled=True)
    swap_x = [(0, 1), (1, 0), (2, 3), (3, 2)]
    swap_y = [(0, 2), (2, 0), (1, 3), (3, 1)]
    w_x = lax.ppermute(w_own, "r", swap_x)
    w_y = lax.ppermute(w_own, "r", swap_y)
    half = groups // 2
    w_d = jnp.concatenate(
        [lax.ppermute(w_x[:half], "r", swap_y), lax.ppermute(w_y[half:], "r", swap_x)], axis=0
    )

    normed = layer_norm(hidden_in, ln_gain, ln_bias)
    x_own = lax.all_to_all(normed, "r", split_axis=0, concat_axis=0, tiled=True)
    x_all = lax.all_gather(x_own, ("z", "c"), axis=0, tiled=False)

    cache_each = cache_kv.shape[1]
    cut = cache_kv.reshape(REQ, cache_each, 2, zs, CORES, cols).transpose(3, 0, 4, 2, 1, 5)
    cached = lax.all_to_all(
        cut.reshape(seq_count, 2, cache_each, cols), seq, split_axis=0, concat_axis=0, tiled=True
    )

    w_out_all = lax.all_gather(w_out, seq, axis=1, tiled=True)

    length = jnp.sum(jnp.where(jnp.arange(REQ) == chip, cache_len, 0))
    new_len = seq_count * new_dev
    cosine, sine = rotary_tables(length + jnp.arange(new_len))
    shape = (zs, REQ, CORES, new_dev, LANES)
    query, keys, values, fresh = project(
        x_all.reshape(groups, REQ, new_dev, depth),
        (w_own, w_x, w_y, w_d),
        cosine.reshape(shape),
        sine.reshape(shape),
        chip,
    )
    flat = (new_len, cols)

    whole = lax.all_to_all(fresh, "r", split_axis=0, concat_axis=0, tiled=True)
    slot_ids = lax.all_gather(slots_of(owner[:, 0], seq_count), ("z", "c"), axis=0, tiled=False)
    slot_ids = slot_ids.reshape(groups, REQ * new_dev)

    attended = attend(
        query.reshape(flat), keys.reshape(flat), values.reshape(flat), cached, length
    )
    back = lax.all_to_all(
        attended.reshape(seq_count, new_dev, cols), seq, split_axis=0, concat_axis=0, tiled=True
    )

    rows = whole.reshape(REQ, groups, new_dev, 2 * cols).transpose(1, 0, 2, 3)
    rows = rows.reshape(groups, REQ * new_dev, 2 * cols)
    placing = (
        jnp.arange(seq_count * SLOTS)[None, :, None] == slot_ids[:, None, :]
    ).astype(jnp.bfloat16)
    outgoing = jnp.einsum("gst,gtw->gsw", placing, rows, preferred_element_type=jnp.float32)
    outgoing = outgoing.astype(jnp.bfloat16).reshape(groups, seq_count, SLOTS, 2 * cols)
    arrived = lax.all_to_all(
        outgoing.transpose(1, 0, 2, 3), seq, split_axis=0, concat_axis=0, tiled=True
    )
    appended = arrived.reshape(zs, REQ, CORES, zs, CORES, SLOTS, 2, cols)
    appended = appended.transpose(3, 1, 4, 5, 6, 0, 2, 7).reshape(seq_count * SLOTS, 2, width)

    rows_back = back.reshape(zs, REQ, CORES, new_dev, cols).transpose(1, 3, 0, 2, 4)
    out = jnp.dot(
        rows_back.reshape(REQ * new_dev, width), w_out_all, preferred_element_type=jnp.float32
    ).astype(jnp.bfloat16)
    return out.reshape(REQ, new_dev, out.shape[1]), appended


def by_tokens(hidden_in, ln_gain, ln_bias, w_qkv, w_out, cache_kv, cache_len, owner):
    new_dev = hidden_in.shape[1]
    tok_rows = REQ * new_dev
    normed = layer_norm(hidden_in.reshape(tok_rows, hidden_in.shape[2]), ln_gain, ln_bias)
    width = w_qkv.shape[2]
    heads_here = width // HD
    seq_count = lax.axis_size("seq")
    seq_here = lax.axis_index("seq")
    cache_each = cache_kv.shape[1]
    cache_dev = REQ * cache_each
    cache_flat = cache_kv.reshape(cache_dev, 2, width)
    rows_dev = cache_dev + tok_rows
    request_ids = jnp.arange(REQ)
    projected = jnp.einsum(
        "tc,icw->itw",
        normed,
        lax.all_gather(w_qkv, "seq", axis=1, tiled=True),
        preferred_element_type=jnp.float32,
    )

    def length_of(requests):
        return jnp.sum(
            jnp.where(requests[:, None] == request_ids[None, :], cache_len[None, :], 0), axis=1
        )

    local_ids = jnp.arange(tok_rows)
    query_req = local_ids // new_dev
    query_pos = length_of(query_req) + seq_here * new_dev + local_ids % new_dev
    shape_heads = (tok_rows, heads_here, HD)
    query = rotate(projected[0].reshape(shape_heads), query_pos).astype(jnp.bfloat16)
    keys_new = (
        rotate(projected[1].reshape(shape_heads), query_pos)
        .astype(jnp.bfloat16)
        .reshape(tok_rows, width)
    )
    values_new = projected[2].astype(jnp.bfloat16)
    fresh = jnp.stack([keys_new, values_new], axis=1)
    local_rows = jnp.concatenate([cache_flat, fresh], axis=0)
    scale_factor = 1.0 / math.sqrt(HD)
    block_rows = lax.all_gather(local_rows, "seq", axis=0, tiled=True)
    count = block_rows.shape[0]
    row_ids = jnp.arange(count)
    source = jnp.floor_divide(row_ids, rows_dev)
    within = row_ids - source * rows_dev
    in_cache = within < cache_dev
    cache_req = jnp.floor_divide(within, cache_each)
    cache_slot = source * cache_each + within - cache_req * cache_each
    new_local = within - cache_dev
    new_req = jnp.floor_divide(new_local, new_dev)
    key_req = jnp.where(in_cache, cache_req, new_req)
    key_len = length_of(key_req)
    key_pos = jnp.where(
        in_cache, cache_slot, key_len + source * new_dev + new_local - new_req * new_dev
    )
    usable = jnp.logical_or(jnp.logical_not(in_cache), cache_slot < key_len)
    allowed = (
        usable[None, :]
        & (key_req[None, :] == query_req[:, None])
        & (key_pos[None, :] <= query_pos[:, None])
    )
    key_rows = block_rows[:, 0].reshape(count, heads_here, HD)
    value_rows = block_rows[:, 1].reshape(count, heads_here, HD)
    scores = (
        jnp.einsum("qhd,khd->hqk", query, key_rows, preferred_element_type=jnp.float32)
        * scale_factor
    )
    scores = jnp.where(allowed[None], scores, MASKED)
    highest = jnp.max(scores, axis=-1)
    weights = jnp.where(allowed[None], jnp.exp(scores - highest[:, :, None]), 0.0)
    weight_sum = jnp.sum(weights, axis=-1)
    weighted = jnp.einsum(
        "hqk,khd->qhd", weights.astype(jnp.bfloat16), value_rows, preferred_element_type=jnp.float32
    )
    attended = (
        (weighted / jnp.transpose(weight_sum)[:, :, None])
        .astype(jnp.bfloat16)
        .reshape(tok_rows, width)
    )
    partial_out = jnp.dot(
        attended,
        lax.all_gather(w_out, "seq", axis=1, tiled=True),
        preferred_element_type=jnp.float32,
    ).astype(jnp.bfloat16)
    summed = (
        lax.psum_scatter(partial_out, "tp", scatter_dimension=1, tiled=True)
        .astype(jnp.float32)
        .astype(jnp.bfloat16)
    )
    attn_out = summed.reshape(REQ, new_dev, summed.shape[1])
    slot_ids = slots_of(owner[:, 0], seq_count)
    placing = (jnp.arange(seq_count * SLOTS)[:, None] == slot_ids[None, :]).astype(jnp.bfloat16)
    outgoing = jnp.einsum("st,tkw->skw", placing, fresh, preferred_element_type=jnp.float32).astype(
        jnp.bfloat16
    )
    outgoing = outgoing.reshape(seq_count, SLOTS, 2, width)
    arrived = lax.all_to_all(outgoing, "seq", split_axis=0, concat_axis=0, tiled=True)
    appended = arrived.reshape(seq_count * SLOTS, 2, width)
    return (attn_out, appended)


def solution(mesh):
    seq_count, tp_count = mesh.shape["seq"], mesh.shape["tp"]
    zs = seq_count // (REQ * CORES)

    def call(*args):
        heads_here = args[3].shape[2] // tp_count // HD
        split = (
            tp_count == 1
            and zs * REQ * CORES == seq_count
            and heads_here % max(zs * CORES, 1) == 0
        )
        if split:
            body, seq, names = by_heads, ("z", "r", "c"), ("z", "r", "c", "tp")
            grid = Mesh(mesh.devices.reshape(zs, REQ, CORES, tp_count), names)
        else:
            body, seq, grid = by_tokens, "seq", mesh
        return jax.shard_map(
            body,
            mesh=grid,
            in_specs=(
                P(None, seq, None),
                P(),
                P(),
                P(None, seq, "tp"),
                P("tp", seq),
                P(None, seq, None, "tp"),
                P(),
                P(seq, None),
            ),
            out_specs=(P(None, seq, "tp"), P(seq, None, "tp")),
            check_vma=False,
        )(*args)

    return call
```

```python
import functools
import math

import jax
import jax.numpy as jnp
from jax import lax
from jax.experimental import pallas as pl
from jax.experimental.pallas import tpu as pltpu
from jax.sharding import Mesh
from jax.sharding import PartitionSpec as P

HD = 256
ROT = 64
REQ = 4
SLOTS = 8
CORES = 2
Z_CHIPS = 4

EPSILON = 1e-05
BASE_FREQ = 10000.0
MASKED = -1e30
LANES = 128


def layer_norm(values_in, gain, shift):
    wide = values_in.astype(jnp.float32)
    center = jnp.mean(wide, axis=-1, keepdims=True)
    spread = wide - center
    variance = jnp.mean(spread * spread, axis=-1, keepdims=True)
    return (spread * lax.rsqrt(variance + EPSILON) * gain + shift).astype(jnp.bfloat16)


def rotate(heads_in, positions):
    pair_index = jnp.arange(ROT // 2).astype(jnp.float32)
    inverse = jnp.power(BASE_FREQ, -2.0 * pair_index / ROT)
    angles = positions.astype(jnp.float32)[:, None] * inverse[None, :]
    cosine = jnp.cos(angles)[:, None, :]
    sine = jnp.sin(angles)[:, None, :]
    leading = heads_in.shape[:-1]
    paired = heads_in[..., :ROT].reshape(leading + (ROT // 2, 2))
    even = paired[..., 0]
    odd = paired[..., 1]
    turned = jnp.stack([even * cosine - odd * sine, odd * cosine + even * sine], axis=-1).reshape(
        leading + (ROT,)
    )
    return jnp.concatenate([turned, heads_in[..., ROT:]], axis=-1)


def rotary_tables(positions):
    lane = jnp.arange(LANES)
    pair_index = (lane // 2).astype(jnp.float32)
    inverse = jnp.power(BASE_FREQ, -2.0 * pair_index / ROT)
    angles = positions.astype(jnp.float32)[:, None] * inverse[None, :]
    turned = lane < ROT
    cosine = jnp.where(turned, jnp.cos(angles), 1.0)
    sine = jnp.where(turned, jnp.where(lane % 2 == 0, -1.0, 1.0) * jnp.sin(angles), 0.0)
    return cosine, sine


def project_kernel(place, *refs):
    q_ref, k_ref, v_ref, send_ref, rows_ref, held, sem_x, sem_w = refs[-8:]
    steps, _, _, each, depth = rows_ref.shape
    weights, (cos_ref, sin_ref) = refs[:10], refs[10:12]
    sources = refs[12 : 12 + 2 * steps]
    groups, _, rows_each, width = weights[0].shape
    zs = groups // CORES
    chip, core, step = place[0], place[1], pl.program_id(0)

    def row_copy(index, c, away):
        return pltpu.make_async_copy(
            sources[2 * index + c].at[away],
            rows_ref.at[index, core ^ c, chip ^ away],
            sem_x.at[index, c, away],
        )

    def weight_copy(which, away, z, c):
        row = pl.multiple_of(((z * REQ + (chip ^ away)) * CORES + c) * rows_each, rows_each)
        group = z * CORES + c
        piece = away + (away == 3 and group >= groups // 2)
        inside = group - groups // 2 if piece == 4 else group
        return pltpu.make_async_copy(
            weights[5 * (which // 2) + piece].at[inside, which % 2],
            held.at[which, pl.ds(row, rows_each)],
            sem_w.at[which, away, group],
        )

    row_parts = [(c, away) for c in range(CORES) for away in range(REQ)]
    weight_parts = [
        (away, z, c) for away in range(REQ) for z in range(zs) for c in range(CORES)
    ]

    @pl.when(step == 0)
    def _():
        for part in row_parts:
            row_copy(0, *part).start()
        for part in weight_parts:
            weight_copy(0, *part).start()

    for index in range(steps):

        @pl.when(step == index)
        def _(index=index):
            for part in row_parts:
                row_copy(index, *part).wait()

    count = CORES * REQ * each
    lane = lax.broadcasted_iota(jnp.int32, (count, LANES), 1)
    even = lane % 2 == 0
    cosine = cos_ref[...].reshape(count, LANES)
    sine = sin_ref[...].reshape(count, LANES)
    for which in range(3):

        @pl.when(step == 0)
        def _(which=which):
            for part in weight_parts:
                weight_copy(which, *part).wait()
            if which < 2:
                for part in weight_parts:
                    weight_copy(which + 1, *part).start()
            else:
                for index in range(1, steps):
                    for part in row_parts:
                        row_copy(index, *part).start()

        rows = rows_ref[step].reshape(count, depth)
        out = jnp.dot(rows, held[which], preferred_element_type=jnp.float32)
        if which < 2:
            pieces = []
            for head in range(width // HD):
                low = out[:, head * HD : head * HD + LANES]
                other = jnp.where(even, pltpu.roll(low, LANES - 1, 1), pltpu.roll(low, 1, 1))
                pieces.append(low * cosine + other * sine)
                pieces.append(out[:, head * HD + LANES : (head + 1) * HD])
            out = jnp.concatenate(pieces, axis=1)
        out = out.astype(jnp.bfloat16).reshape(CORES, REQ, each, width)
        for c in range(CORES):
            for r in range(REQ):
                part = out[c, r]
                if which == 0:
                    q_ref[0, r, c] = part
                elif which == 1:
                    k_ref[0, r, c] = part
                    send_ref[r ^ chip, 0, c, :, :width] = part
                else:
                    v_ref[0, r, c] = part
                    send_ref[r ^ chip, 0, c, :, width:] = part


def project(x_pairs, weights, cosine, sine, place, held, cost):
    steps = len(x_pairs) // CORES
    _, each, depth = x_pairs[0].shape
    groups, _, rows_each, width = weights[0].shape
    zs = groups // CORES
    table = pl.BlockSpec((1, CORES, REQ, each, LANES), lambda i, s: (s[2 + i], 0, 0, 0, 0))
    token = pl.BlockSpec((1, REQ, CORES, each, width), lambda i, s: (s[2 + i], 0, 0, 0, 0))
    whole = jax.ShapeDtypeStruct((zs, REQ, CORES, each, width), jnp.bfloat16)
    anywhere = pl.BlockSpec(memory_space=pl.ANY)
    return pl.pallas_call(
        project_kernel,
        grid_spec=pltpu.PrefetchScalarGridSpec(
            num_scalar_prefetch=1,
            grid=(steps,),
            in_specs=[anywhere] * len(weights)
            + [table, table]
            + [anywhere] * (len(x_pairs) + len(held)),
            out_specs=[
                token,
                token,
                token,
                pl.BlockSpec(
                    (REQ, 1, CORES, each, 2 * width), lambda i, s: (0, i, 0, 0, 0)
                ),
            ],
            scratch_shapes=[
                pltpu.VMEM((steps, CORES, REQ, each, depth), jnp.bfloat16),
                pltpu.VMEM((3, depth, width), jnp.bfloat16),
                pltpu.SemaphoreType.DMA((steps, CORES, REQ)),
                pltpu.SemaphoreType.DMA((3, REQ, groups)),
            ],
        ),
        out_shape=[
            whole,
            whole,
            whole,
            jax.ShapeDtypeStruct((REQ, steps, CORES, each, 2 * width), jnp.bfloat16),
        ],
        input_output_aliases={3 + len(weights) + len(x_pairs) + i: i for i in range(len(held))},
        compiler_params=pltpu.CompilerParams(
            vmem_limit_bytes=58 * 2**20, dimension_semantics=("arbitrary",)
        ),
        cost_estimate=pl.CostEstimate(
            flops=2 * steps * CORES * REQ * each * depth * 3 * width * cost,
            bytes_accessed=2 * (x_pairs[0].size * len(x_pairs) + 3 * depth * width) * cost,
            transcendentals=0,
        ),
    )(place, *weights, cosine, sine, *x_pairs, *held)


def order_kernel(blocks, slot_ref, *refs):
    out_ref = refs[-1]
    owners = out_ref.shape[0]
    count = slot_ref.shape[3]
    wanted = lax.broadcasted_iota(jnp.int32, (owners * SLOTS, count), 0)
    index = 0
    for call in range(len(refs) // REQ):
        parts = refs[call * REQ : (call + 1) * REQ]
        for step in range(parts[0].shape[0]):
            ordered = []
            for c in range(CORES):
                placing = (wanted == slot_ref[index, c]).astype(jnp.bfloat16)
                rows = jnp.concatenate([part[step, c] for part in parts], axis=0)
                out = jnp.dot(placing, rows, preferred_element_type=jnp.float32)
                ordered.append(out.reshape(owners, SLOTS, rows.shape[1]))
            both = jnp.concatenate(ordered, axis=1).astype(jnp.bfloat16)
            out_ref[:, pl.ds(blocks[index], 1)] = both[:, None]
            index += 1


def order(blocks, slot_ids, parts, owners):
    zs = slot_ids.shape[0]
    each, wide = parts[0].shape[-2:]
    out = (owners, zs, CORES * SLOTS, wide)
    return pl.pallas_call(
        order_kernel,
        grid_spec=pltpu.PrefetchScalarGridSpec(
            num_scalar_prefetch=1,
            grid=(1,),
            in_specs=[pl.BlockSpec(slot_ids.shape, lambda i, s: (0, 0, 0, 0))]
            + [pl.BlockSpec(part.shape, lambda i, s: (0, 0, 0, 0)) for part in parts],
            out_specs=pl.BlockSpec(out, lambda i, s: (0, 0, 0, 0)),
        ),
        out_shape=jax.ShapeDtypeStruct(out, jnp.bfloat16),
        compiler_params=pltpu.CompilerParams(
            vmem_limit_bytes=56 * 2**20, dimension_semantics=("arbitrary",)
        ),
        cost_estimate=pl.CostEstimate(
            flops=2 * zs * CORES * (owners * SLOTS) * REQ * each * wide,
            bytes_accessed=4 * owners * zs * CORES * SLOTS * wide,
            transcendentals=0,
        ),
    )(blocks, slot_ids, *parts)


def attend_kernel(length, q_ref, k_ref, v_ref, kc_ref, vc_ref, o_ref, *, blocks):
    step = pl.program_id(1)
    size = q_ref.shape[0]
    factor = math.log2(math.e) / math.sqrt(HD)
    contract = (((1,), (1,)), ((), ()))
    slots = kc_ref.shape[0] * kc_ref.shape[1]

    for index in range(blocks):

        @pl.when(step == index)
        def _(index=index):
            query = q_ref[...]
            k_old = kc_ref[...].reshape(slots, HD)
            v_old = vc_ref[...].reshape(slots, HD)
            old = lax.dot_general(query, k_old, contract, preferred_element_type=jnp.float32)
            slot = lax.broadcasted_iota(jnp.int32, old.shape, 1)
            old = jnp.where(slot < length[0], old, MASKED)
            parts = [(old, v_old)]
            if index:
                span = index * size
                parts.append(
                    (
                        lax.dot_general(
                            query, k_ref[:span], contract, preferred_element_type=jnp.float32
                        ),
                        v_ref[:span],
                    )
                )
            own = lax.dot_general(
                query,
                k_ref[index * size : (index + 1) * size],
                contract,
                preferred_element_type=jnp.float32,
            )
            row = lax.broadcasted_iota(jnp.int32, own.shape, 0)
            column = lax.broadcasted_iota(jnp.int32, own.shape, 1)
            own = jnp.where(column <= row, own, MASKED)
            parts.append((own, v_ref[index * size : (index + 1) * size]))
            highest = functools.reduce(
                jnp.maximum, [jnp.max(s, axis=1, keepdims=True) for s, _ in parts]
            )
            total, mixed = 0.0, 0.0
            for scores, values in parts:
                weights = jnp.exp2((scores - highest) * factor)
                total = total + jnp.sum(weights, axis=1, keepdims=True)
                mixed = mixed + jnp.dot(
                    weights.astype(jnp.bfloat16), values, preferred_element_type=jnp.float32
                )
            o_ref[...] = (mixed / total).astype(jnp.bfloat16)


def attend(query, keys, values, cached, length):
    count, width = query.shape
    heads, size = width // HD, min(256, count)
    blocks = count // size
    sources, _, each, _ = cached.shape

    def old(which):
        return pl.BlockSpec((sources, None, each, HD), lambda h, i, s: (0, which, 0, h))

    return pl.pallas_call(
        functools.partial(attend_kernel, blocks=blocks),
        grid_spec=pltpu.PrefetchScalarGridSpec(
            num_scalar_prefetch=1,
            grid=(heads, blocks),
            in_specs=[
                pl.BlockSpec((size, HD), lambda h, i, s: (i, h)),
                pl.BlockSpec((count, HD), lambda h, i, s: (0, h)),
                pl.BlockSpec((count, HD), lambda h, i, s: (0, h)),
                old(0),
                old(1),
            ],
            out_specs=pl.BlockSpec((size, HD), lambda h, i, s: (i, h)),
        ),
        out_shape=jax.ShapeDtypeStruct((count, width), jnp.bfloat16),
        compiler_params=pltpu.CompilerParams(
            vmem_limit_bytes=48 * 2**20, dimension_semantics=("arbitrary", "arbitrary")
        ),
        cost_estimate=pl.CostEstimate(
            flops=4 * count * (count // 2 + sources * each) * width,
            bytes_accessed=2 * 4 * count * width,
            transcendentals=count * (count // 2 + sources * each) * heads,
        ),
    )(jnp.reshape(length, (1,)), query, keys, values, cached, cached)


def output_kernel(place, *refs):
    mine_ref, other_ref, lhs, held, sem_l, sem_w = refs[-6:]
    sources, weights = refs[:CORES], refs[CORES:-6]
    zs = lhs.shape[3] // (sources[0].shape[2] * CORES)
    each, cols = sources[0].shape[1:]
    lanes = weights[0].shape[2]
    depth = lhs.shape[3]
    chip, step = place[0], pl.program_id(0)

    def row_copy(which, z, r, c):
        source = (z * REQ + r) * CORES + c
        return pltpu.make_async_copy(
            sources[which].at[source],
            lhs.at[which, r, :, pl.ds((z * CORES + c) * cols, cols)],
            sem_l.at[which, source],
        )

    row_parts = [
        (which, z, r, c)
        for which in range(CORES)
        for z in range(zs)
        for r in range(REQ)
        for c in range(CORES)
    ]

    def weight_copies(index, r):
        column = pl.multiple_of((chip ^ r) * lanes, lanes)
        if index == 0:
            pairs = [(weights[0].at[r], held.at[0, :, pl.ds(r * lanes, lanes)])]
        elif index == 1:
            half = depth // 2
            pairs = [
                (
                    weights[4 + part].at[0] if r == 3 else weights[1 + r].at[part],
                    held.at[1, pl.ds(part * half, half), pl.ds(column, lanes)],
                )
                for part in range(2)
            ]
        else:
            part = index - 2
            source = weights[9 + part].at[0] if r == 3 else weights[6 + r].at[part]
            pairs = [(source, held.at[index, :, pl.ds(column, lanes)])]
        return [
            pltpu.make_async_copy(source, target, sem_w.at[index, r, number])
            for number, (source, target) in enumerate(pairs)
        ]

    @pl.when(step == 0)
    def _():
        for part in row_parts:
            row_copy(*part).start()
        for index in range(zs):
            for r in range(REQ):
                for copy in weight_copies(index, r):
                    copy.start()
        for part in row_parts:
            row_copy(*part).wait()

    for index in range(zs):

        @pl.when(step == index)
        def _(index=index):
            for r in range(REQ):
                for copy in weight_copies(index, r):
                    copy.wait()

    rows = lhs[...].reshape(CORES * REQ * each, depth)
    out = jnp.dot(rows, held[step], preferred_element_type=jnp.float32).astype(jnp.bfloat16)
    mine_ref[...] = out[: REQ * each]
    other_ref[...] = out[REQ * each :]


def output(place, back, back_other, weights):
    sources, each, cols = back.shape
    _, depth, lanes = weights[0].shape
    zs = sources // (REQ * CORES)
    anywhere = pl.BlockSpec(memory_space=pl.ANY)
    block = pl.BlockSpec((REQ * each, REQ * lanes), lambda i, s: (0, s[1 + i]))
    shape = jax.ShapeDtypeStruct((REQ * each, zs * REQ * lanes), jnp.bfloat16)
    return pl.pallas_call(
        output_kernel,
        grid_spec=pltpu.PrefetchScalarGridSpec(
            num_scalar_prefetch=1,
            grid=(zs,),
            in_specs=[anywhere] * (CORES + len(weights)),
            out_specs=[block, block],
            scratch_shapes=[
                pltpu.VMEM((CORES, REQ, each, depth), jnp.bfloat16),
                pltpu.VMEM((zs, depth, REQ * lanes), jnp.bfloat16),
                pltpu.SemaphoreType.DMA((CORES, sources)),
                pltpu.SemaphoreType.DMA((zs, REQ, 2)),
            ],
        ),
        out_shape=[shape, shape],
        compiler_params=pltpu.CompilerParams(
            vmem_limit_bytes=56 * 2**20, dimension_semantics=("arbitrary",)
        ),
        cost_estimate=pl.CostEstimate(
            flops=2 * CORES * REQ * each * depth * zs * REQ * lanes,
            bytes_accessed=2 * (2 * back.size + depth * zs * REQ * lanes),
            transcendentals=0,
        ),
    )(place, back, back_other, *weights)


def interleave_kernel(place, mine_ref, other_ref, out_ref):
    lanes = LANES
    core = place[0]
    for block in range(mine_ref.shape[1] // lanes):
        part = slice(block * lanes, (block + 1) * lanes)
        here = pl.multiple_of((CORES * block + core) * lanes, lanes)
        there = pl.multiple_of((CORES * block + 1 - core) * lanes, lanes)
        out_ref[:, pl.ds(here, lanes)] = mine_ref[:, part]
        out_ref[:, pl.ds(there, lanes)] = other_ref[:, part]


def interleave(core, mine, other):
    rows, width = mine.shape
    tile = pl.BlockSpec((rows, width // 2), lambda i, s: (0, i))
    return pl.pallas_call(
        interleave_kernel,
        grid_spec=pltpu.PrefetchScalarGridSpec(
            num_scalar_prefetch=1,
            grid=(2,),
            in_specs=[tile, tile],
            out_specs=pl.BlockSpec((rows, width), lambda i, s: (0, i)),
        ),
        out_shape=jax.ShapeDtypeStruct((rows, CORES * width), mine.dtype),
        compiler_params=pltpu.CompilerParams(dimension_semantics=("arbitrary",)),
        cost_estimate=pl.CostEstimate(
            flops=0, bytes_accessed=8 * rows * width, transcendentals=0
        ),
    )(jnp.reshape(core, (1,)), mine, other)


def slots_of(owners, count):
    marks = (owners[:, None] == jnp.arange(count)[None, :]).astype(jnp.int32)
    earlier = jnp.cumsum(marks, axis=0) - marks
    return owners * SLOTS + jnp.sum(earlier * marks, axis=1)


def swap_chips(value, away):
    return lax.ppermute(value, "r", [(chip, chip ^ away) for chip in range(REQ)])


def swap_cores(value):
    return lax.ppermute(value, "c", [(0, 1), (1, 0)])


def z_step(up, down, step):
    last = Z_CHIPS - 1
    up = lax.ppermute(up, "z", [(z, z + 1) for z in range(step, last)])
    down = lax.ppermute(down, "z", [(z, z - 1) for z in range(1, Z_CHIPS - step)])
    return up, down


def by_block(z, steps, column):
    up, down = zip(*steps)
    if column == 1:
        return jnp.where(z == 0, down[0], up[0])
    if column == 2:
        return jnp.where(z == 0, down[1], jnp.where(z == 3, up[1], down[0]))
    return jnp.where(
        z == 0, down[2], jnp.where(z == 1, down[1], jnp.where(z == 2, up[1], up[2]))
    )


def block_table():
    return jnp.array([[0, 1, 2, 3], [1, 0, 2, 3], [2, 1, 3, 0], [3, 2, 1, 0]], jnp.int32)


def by_heads(hidden_in, ln_gain, ln_bias, w_qkv, w_out, cache_kv, cache_len, owner):
    zs, seq_count = lax.axis_size("z"), lax.axis_size("z") * REQ * CORES
    groups = zs * CORES
    z, chip, core = lax.axis_index("z"), lax.axis_index("r"), lax.axis_index("c")
    seq = ("z", "r", "c")
    new_dev, depth = hidden_in.shape[1], hidden_in.shape[2]
    width = w_qkv.shape[2]
    cols = width // groups
    blocks = block_table()[z]

    def near(part):
        return part + (swap_chips(part[0], 1), swap_chips(part[0], 2))

    def far(part):
        half = part[1].shape[0] // 2
        return part + (swap_chips(part[1][:half], 2), swap_chips(part[2][half:], 1))

    rows_dev = w_qkv.shape[1]
    w_cut = w_qkv.reshape(3, rows_dev, groups, cols).transpose(2, 0, 1, 3)
    slots_here = slots_of(owner[:, 0], seq_count).astype(jnp.bfloat16)
    slot_rows = jnp.zeros((groups, 8, cols), jnp.bfloat16)
    slot_rows = slot_rows.at[:, 0, : slots_here.shape[0]].set(slots_here[None])
    w_cut = jnp.concatenate([w_cut.reshape(groups, 3 * rows_dev, cols), slot_rows], axis=1)
    w_cut = lax.all_to_all(w_cut, ("z", "c"), split_axis=0, concat_axis=0, tiled=True)

    normed = layer_norm(hidden_in, ln_gain, ln_bias)
    x_own = jnp.stack(
        [
            swap_chips(lax.dynamic_index_in_dim(normed, chip ^ away, 0, keepdims=False), away)
            if away
            else lax.dynamic_index_in_dim(normed, chip, 0, keepdims=False)
            for away in range(REQ)
        ]
    )
    cache_each = cache_kv.shape[1]
    cut = cache_kv.reshape(REQ, cache_each, 2, zs, CORES, cols).transpose(3, 0, 4, 2, 1, 5)
    cut = cut.reshape(seq_count, 2, cache_each, cols)

    length = jnp.sum(jnp.where(jnp.arange(REQ) == chip, cache_len, 0))
    new_len = seq_count * new_dev
    cosine, sine = rotary_tables(length + jnp.arange(new_len))
    shape = (zs, REQ, CORES, new_dev, LANES)
    tables = [table.reshape(shape).transpose(0, 2, 1, 3, 4) for table in (cosine, sine)]

    x_own, w_cut = lax.optimization_barrier((x_own, w_cut))
    w_own = w_cut[:, : 3 * rows_dev].reshape(groups, 3, rows_dev, cols)
    slot_ids = w_cut[:, 3 * rows_dev, : slots_here.shape[0]].astype(jnp.int32)
    slot_ids = slot_ids.reshape(zs, CORES, REQ, new_dev)[blocks]
    slot_ids = slot_ids[:, :, chip ^ jnp.arange(REQ)].reshape(zs, CORES, 1, REQ * new_dev)

    out_parts = [lax.all_gather(w_out, "r", axis=0, tiled=False)]

    w_parts = [(w_own[:, :2],), (w_own[:, 2:],)]
    x_steps = [z_step(x_own, x_own, 0)]
    other_own = swap_cores(x_own)
    w_parts = [near(w_parts[0]), w_parts[1]]
    x_steps, w_parts, other_own, tables, out_parts = lax.optimization_barrier(
        (x_steps, w_parts, other_own, tables, out_parts)
    )
    x_steps = x_steps + [z_step(*x_steps[0], 1)]
    x_first = by_block(z, x_steps, 1)
    other_first = swap_cores(x_first)
    w_parts = [far(w_parts[0]), near(w_parts[1])]
    x_steps, w_parts, x_first, other_first = lax.optimization_barrier(
        (x_steps, w_parts, x_first, other_first)
    )
    x_steps = x_steps + [z_step(*x_steps[1], 2)]
    x_second = by_block(z, x_steps, 2)
    other_second = swap_cores(x_second)
    w_parts = [w_parts[0], far(w_parts[1])]
    weights = [piece for part in w_parts for piece in part]

    def run(first, pairs, held, cost):
        steps = len(pairs) // CORES
        place = jnp.concatenate([jnp.stack([chip, core]), blocks[first : first + steps]])
        *held, fresh = project(pairs, weights, *tables, place.astype(jnp.int32), held, cost)
        return held, fresh

    def send(fresh):
        return [fresh[0]] + [swap_chips(fresh[away], away) for away in range(1, REQ)]

    held, fresh = run(0, [x_own, other_own, x_first, other_first], (), 0)
    x_steps, held, fresh, x_second, other_second, w_out = lax.optimization_barrier(
        (x_steps, held, fresh, x_second, other_second, w_out)
    )
    out_steps = [z_step(w_out, w_out, 0)]
    x_last = by_block(z, x_steps, 3)
    sent = send(fresh)
    cached = lax.all_to_all(cut, seq, split_axis=0, concat_axis=0, tiled=True)
    held, fresh = run(2, [x_second, other_second, x_last, swap_cores(x_last)], held, 1)
    out_steps, sent, held, fresh, cached = lax.optimization_barrier(
        (out_steps, sent, held, fresh, cached)
    )
    w_first = by_block(z, out_steps, 1)
    w_first = far(near((w_first.reshape(2, w_first.shape[0] // 2, w_first.shape[1]),)))
    out_steps += [z_step(*out_steps[0], 1)]
    out_steps += [z_step(*out_steps[1], 2)]
    sent += send(fresh)
    query, keys, values = held
    flat = (new_len, cols)

    attended = attend(
        query.reshape(flat), keys.reshape(flat), values.reshape(flat), cached, length
    )
    out_steps, attended, sent, w_first = lax.optimization_barrier(
        (out_steps, attended, sent, w_first)
    )
    out_parts += w_first
    rest = near((jnp.stack([by_block(z, out_steps, 2), by_block(z, out_steps, 3)]),))
    back = lax.all_to_all(
        attended.reshape(seq_count, new_dev, cols), seq, split_axis=0, concat_axis=0, tiled=True
    )
    outgoing = order(blocks, slot_ids, sent, seq_count)
    back, outgoing, rest = lax.optimization_barrier((back, outgoing, rest))
    out_parts += far(rest)
    arrived = lax.all_to_all(outgoing, seq, split_axis=0, concat_axis=0, tiled=True)
    appended = arrived.reshape(zs, REQ, CORES, zs, CORES, SLOTS, 2, cols)
    appended = appended.transpose(3, 1, 4, 5, 6, 0, 2, 7).reshape(seq_count * SLOTS, 2, width)

    place = jnp.concatenate([jnp.stack([chip]), blocks]).astype(jnp.int32)
    out, out_other = output(place, back, swap_cores(back), out_parts)
    out = interleave(core, out, swap_cores(out_other))
    return out.reshape(REQ, new_dev, out.shape[1]), appended


def by_tokens(hidden_in, ln_gain, ln_bias, w_qkv, w_out, cache_kv, cache_len, owner):
    new_dev = hidden_in.shape[1]
    tok_rows = REQ * new_dev
    normed = layer_norm(hidden_in.reshape(tok_rows, hidden_in.shape[2]), ln_gain, ln_bias)
    width = w_qkv.shape[2]
    heads_here = width // HD
    seq_count = lax.axis_size("seq")
    seq_here = lax.axis_index("seq")
    cache_each = cache_kv.shape[1]
    cache_dev = REQ * cache_each
    cache_flat = cache_kv.reshape(cache_dev, 2, width)
    rows_dev = cache_dev + tok_rows
    request_ids = jnp.arange(REQ)
    projected = jnp.einsum(
        "tc,icw->itw",
        normed,
        lax.all_gather(w_qkv, "seq", axis=1, tiled=True),
        preferred_element_type=jnp.float32,
    )

    def length_of(requests):
        return jnp.sum(
            jnp.where(requests[:, None] == request_ids[None, :], cache_len[None, :], 0), axis=1
        )

    local_ids = jnp.arange(tok_rows)
    query_req = local_ids // new_dev
    query_pos = length_of(query_req) + seq_here * new_dev + local_ids % new_dev
    shape_heads = (tok_rows, heads_here, HD)
    query = rotate(projected[0].reshape(shape_heads), query_pos).astype(jnp.bfloat16)
    keys_new = (
        rotate(projected[1].reshape(shape_heads), query_pos)
        .astype(jnp.bfloat16)
        .reshape(tok_rows, width)
    )
    values_new = projected[2].astype(jnp.bfloat16)
    fresh = jnp.stack([keys_new, values_new], axis=1)
    local_rows = jnp.concatenate([cache_flat, fresh], axis=0)
    scale_factor = 1.0 / math.sqrt(HD)
    block_rows = lax.all_gather(local_rows, "seq", axis=0, tiled=True)
    count = block_rows.shape[0]
    row_ids = jnp.arange(count)
    source = jnp.floor_divide(row_ids, rows_dev)
    within = row_ids - source * rows_dev
    in_cache = within < cache_dev
    cache_req = jnp.floor_divide(within, cache_each)
    cache_slot = source * cache_each + within - cache_req * cache_each
    new_local = within - cache_dev
    new_req = jnp.floor_divide(new_local, new_dev)
    key_req = jnp.where(in_cache, cache_req, new_req)
    key_len = length_of(key_req)
    key_pos = jnp.where(
        in_cache, cache_slot, key_len + source * new_dev + new_local - new_req * new_dev
    )
    usable = jnp.logical_or(jnp.logical_not(in_cache), cache_slot < key_len)
    allowed = (
        usable[None, :]
        & (key_req[None, :] == query_req[:, None])
        & (key_pos[None, :] <= query_pos[:, None])
    )
    key_rows = block_rows[:, 0].reshape(count, heads_here, HD)
    value_rows = block_rows[:, 1].reshape(count, heads_here, HD)
    scores = (
        jnp.einsum("qhd,khd->hqk", query, key_rows, preferred_element_type=jnp.float32)
        * scale_factor
    )
    scores = jnp.where(allowed[None], scores, MASKED)
    highest = jnp.max(scores, axis=-1)
    weights = jnp.where(allowed[None], jnp.exp(scores - highest[:, :, None]), 0.0)
    weight_sum = jnp.sum(weights, axis=-1)
    weighted = jnp.einsum(
        "hqk,khd->qhd", weights.astype(jnp.bfloat16), value_rows, preferred_element_type=jnp.float32
    )
    attended = (
        (weighted / jnp.transpose(weight_sum)[:, :, None])
        .astype(jnp.bfloat16)
        .reshape(tok_rows, width)
    )
    partial_out = jnp.dot(
        attended,
        lax.all_gather(w_out, "seq", axis=1, tiled=True),
        preferred_element_type=jnp.float32,
    ).astype(jnp.bfloat16)
    summed = (
        lax.psum_scatter(partial_out, "tp", scatter_dimension=1, tiled=True)
        .astype(jnp.float32)
        .astype(jnp.bfloat16)
    )
    attn_out = summed.reshape(REQ, new_dev, summed.shape[1])
    slot_ids = slots_of(owner[:, 0], seq_count)
    placing = (jnp.arange(seq_count * SLOTS)[:, None] == slot_ids[None, :]).astype(jnp.bfloat16)
    outgoing = jnp.einsum("st,tkw->skw", placing, fresh, preferred_element_type=jnp.float32).astype(
        jnp.bfloat16
    )
    outgoing = outgoing.reshape(seq_count, SLOTS, 2, width)
    arrived = lax.all_to_all(outgoing, "seq", split_axis=0, concat_axis=0, tiled=True)
    appended = arrived.reshape(seq_count * SLOTS, 2, width)
    return (attn_out, appended)


def solution(mesh):
    seq_count, tp_count = mesh.shape["seq"], mesh.shape["tp"]
    zs = seq_count // (REQ * CORES)

    def call(*args):
        heads_here = args[3].shape[2] // tp_count // HD
        split = (
            tp_count == 1
            and zs == Z_CHIPS
            and zs * REQ * CORES == seq_count
            and heads_here % max(zs * CORES, 1) == 0
        )
        if split:
            body, seq, names = by_heads, ("z", "r", "c"), ("z", "r", "c", "tp")
            grid = Mesh(mesh.devices.reshape(zs, REQ, CORES, tp_count), names)
        else:
            body, seq, grid = by_tokens, "seq", mesh
        return jax.shard_map(
            body,
            mesh=grid,
            in_specs=(
                P(None, seq, None),
                P(),
                P(),
                P(None, seq, "tp"),
                P("tp", seq),
                P(None, seq, None, "tp"),
                P(),
                P(seq, None),
            ),
            out_specs=(P(None, seq, "tp"), P(seq, None, "tp")),
            check_vma=False,
        )(*args)

    return call
```

```python
import functools
import math

import jax
import jax.numpy as jnp
from jax import lax
from jax.experimental import pallas as pl
from jax.experimental.pallas import tpu as pltpu
from jax.sharding import Mesh
from jax.sharding import PartitionSpec as P

HD = 256
ROT = 64
REQ = 4
SLOTS = 8
CORES = 2
Z_CHIPS = 4

EPSILON = 1e-05
BASE_FREQ = 10000.0
MASKED = -1e30
LANES = 128


def layer_norm(values_in, gain, shift):
    wide = values_in.astype(jnp.float32)
    center = jnp.mean(wide, axis=-1, keepdims=True)
    spread = wide - center
    variance = jnp.mean(spread * spread, axis=-1, keepdims=True)
    return (spread * lax.rsqrt(variance + EPSILON) * gain + shift).astype(jnp.bfloat16)


def rotate(heads_in, positions):
    pair_index = jnp.arange(ROT // 2).astype(jnp.float32)
    inverse = jnp.power(BASE_FREQ, -2.0 * pair_index / ROT)
    angles = positions.astype(jnp.float32)[:, None] * inverse[None, :]
    cosine = jnp.cos(angles)[:, None, :]
    sine = jnp.sin(angles)[:, None, :]
    leading = heads_in.shape[:-1]
    paired = heads_in[..., :ROT].reshape(leading + (ROT // 2, 2))
    even = paired[..., 0]
    odd = paired[..., 1]
    turned = jnp.stack([even * cosine - odd * sine, odd * cosine + even * sine], axis=-1).reshape(
        leading + (ROT,)
    )
    return jnp.concatenate([turned, heads_in[..., ROT:]], axis=-1)


def rotary_tables(positions):
    lane = jnp.arange(LANES)
    pair_index = (lane // 2).astype(jnp.float32)
    inverse = jnp.power(BASE_FREQ, -2.0 * pair_index / ROT)
    angles = positions.astype(jnp.float32)[:, None] * inverse[None, :]
    turned = lane < ROT
    cosine = jnp.where(turned, jnp.cos(angles), 1.0)
    sine = jnp.where(turned, jnp.where(lane % 2 == 0, -1.0, 1.0) * jnp.sin(angles), 0.0)
    return cosine, sine


def project_kernel(place, *refs, by_chip):
    q_ref, k_ref, v_ref, send_ref, rows_ref, held, sem_x, sem_w = refs[-8:]
    steps, _, _, each, depth = rows_ref.shape
    weights, (cos_ref, sin_ref) = refs[:10], refs[10:12]
    sources = refs[12 : 12 + 2 * steps]
    groups, _, rows_each, width = weights[0].shape
    zs = groups // CORES
    chip, core, step = place[0], place[1], pl.program_id(0)

    def row_copy(index, c, away):
        return pltpu.make_async_copy(
            sources[2 * index + c].at[away],
            rows_ref.at[index, core ^ c, chip ^ away],
            sem_x.at[index, c, away],
        )

    def weight_copy(which, away, z, c):
        row = pl.multiple_of(((z * REQ + (chip ^ away)) * CORES + c) * rows_each, rows_each)
        group = z * CORES + c
        piece = away + (away == 3 and group >= groups // 2)
        inside = group - groups // 2 if piece == 4 else group
        return pltpu.make_async_copy(
            weights[5 * (which // 2) + piece].at[inside, which % 2],
            held.at[which, pl.ds(row, rows_each)],
            sem_w.at[which, away, group],
        )

    row_parts = [(c, away) for c in range(CORES) for away in range(REQ)]
    weight_parts = [
        (away, z, c) for away in range(REQ) for z in range(zs) for c in range(CORES)
    ]

    @pl.when(step == 0)
    def _():
        for part in row_parts:
            row_copy(0, *part).start()
        for part in weight_parts:
            weight_copy(0, *part).start()

    for index in range(steps):

        @pl.when(step == index)
        def _(index=index):
            for part in row_parts:
                row_copy(index, *part).wait()

    count = CORES * REQ * each
    lane = lax.broadcasted_iota(jnp.int32, (count, LANES), 1)
    even = lane % 2 == 0
    cosine = cos_ref[...].reshape(count, LANES)
    sine = sin_ref[...].reshape(count, LANES)
    for which in range(3):

        @pl.when(step == 0)
        def _(which=which):
            for part in weight_parts:
                weight_copy(which, *part).wait()
            if which < 2:
                for part in weight_parts:
                    weight_copy(which + 1, *part).start()
            else:
                for index in range(1, steps):
                    for part in row_parts:
                        row_copy(index, *part).start()

        rows = rows_ref[step].reshape(count, depth)
        out = jnp.dot(rows, held[which], preferred_element_type=jnp.float32)
        if which < 2:
            pieces = []
            for head in range(width // HD):
                low = out[:, head * HD : head * HD + LANES]
                other = jnp.where(even, pltpu.roll(low, LANES - 1, 1), pltpu.roll(low, 1, 1))
                pieces.append(low * cosine + other * sine)
                pieces.append(out[:, head * HD + LANES : (head + 1) * HD])
            out = jnp.concatenate(pieces, axis=1)
        out = out.astype(jnp.bfloat16).reshape(CORES, REQ, each, width)
        for c in range(CORES):
            for r in range(REQ):
                part = out[c, r]
                if which == 0:
                    q_ref[0, r, c] = part
                elif which == 1:
                    k_ref[0, r, c] = part
                    send_ref[r if by_chip else r ^ chip, 0, c, :, :width] = part
                else:
                    v_ref[0, r, c] = part
                    send_ref[r if by_chip else r ^ chip, 0, c, :, width:] = part


def project(x_pairs, weights, cosine, sine, place, held, cost, by_chip):
    steps = len(x_pairs) // CORES
    _, each, depth = x_pairs[0].shape
    groups, _, rows_each, width = weights[0].shape
    zs = groups // CORES
    table = pl.BlockSpec((1, CORES, REQ, each, LANES), lambda i, s: (s[2 + i], 0, 0, 0, 0))
    token = pl.BlockSpec((1, REQ, CORES, each, width), lambda i, s: (s[2 + i], 0, 0, 0, 0))
    whole = jax.ShapeDtypeStruct((zs, REQ, CORES, each, width), jnp.bfloat16)
    anywhere = pl.BlockSpec(memory_space=pl.ANY)
    return pl.pallas_call(
        functools.partial(project_kernel, by_chip=by_chip),
        grid_spec=pltpu.PrefetchScalarGridSpec(
            num_scalar_prefetch=1,
            grid=(steps,),
            in_specs=[anywhere] * len(weights)
            + [table, table]
            + [anywhere] * (len(x_pairs) + len(held)),
            out_specs=[
                token,
                token,
                token,
                pl.BlockSpec(
                    (REQ, 1, CORES, each, 2 * width), lambda i, s: (0, i, 0, 0, 0)
                ),
            ],
            scratch_shapes=[
                pltpu.VMEM((steps, CORES, REQ, each, depth), jnp.bfloat16),
                pltpu.VMEM((3, depth, width), jnp.bfloat16),
                pltpu.SemaphoreType.DMA((steps, CORES, REQ)),
                pltpu.SemaphoreType.DMA((3, REQ, groups)),
            ],
        ),
        out_shape=[
            whole,
            whole,
            whole,
            jax.ShapeDtypeStruct((REQ, steps, CORES, each, 2 * width), jnp.bfloat16),
        ],
        input_output_aliases={3 + len(weights) + len(x_pairs) + i: i for i in range(len(held))},
        compiler_params=pltpu.CompilerParams(
            vmem_limit_bytes=58 * 2**20, dimension_semantics=("arbitrary",)
        ),
        cost_estimate=pl.CostEstimate(
            flops=2 * steps * CORES * REQ * each * depth * 3 * width * cost,
            bytes_accessed=2 * (x_pairs[0].size * len(x_pairs) + 3 * depth * width) * cost,
            transcendentals=0,
        ),
    )(place, *weights, cosine, sine, *x_pairs, *held)


def order_kernel(blocks, slot_ref, *refs):
    out_ref = refs[-1]
    owners = out_ref.shape[0]
    count = slot_ref.shape[3]
    wanted = lax.broadcasted_iota(jnp.int32, (owners * SLOTS, count), 0)
    index = 0
    for call in range(len(refs) // REQ):
        parts = refs[call * REQ : (call + 1) * REQ]
        for step in range(parts[0].shape[0]):
            ordered = []
            for c in range(CORES):
                placing = (wanted == slot_ref[index, c]).astype(jnp.bfloat16)
                rows = jnp.concatenate([part[step, c] for part in parts], axis=0)
                out = jnp.dot(placing, rows, preferred_element_type=jnp.float32)
                ordered.append(out.reshape(owners, SLOTS, rows.shape[1]))
            both = jnp.concatenate(ordered, axis=1).astype(jnp.bfloat16)
            out_ref[:, pl.ds(blocks[index], 1)] = both[:, None]
            index += 1


def order(blocks, slot_ids, parts, owners):
    zs = slot_ids.shape[0]
    each, wide = parts[0].shape[-2:]
    out = (owners, zs, CORES * SLOTS, wide)
    return pl.pallas_call(
        order_kernel,
        grid_spec=pltpu.PrefetchScalarGridSpec(
            num_scalar_prefetch=1,
            grid=(1,),
            in_specs=[pl.BlockSpec(slot_ids.shape, lambda i, s: (0, 0, 0, 0))]
            + [pl.BlockSpec(part.shape, lambda i, s: (0, 0, 0, 0)) for part in parts],
            out_specs=pl.BlockSpec(out, lambda i, s: (0, 0, 0, 0)),
        ),
        out_shape=jax.ShapeDtypeStruct(out, jnp.bfloat16),
        compiler_params=pltpu.CompilerParams(
            vmem_limit_bytes=56 * 2**20, dimension_semantics=("arbitrary",)
        ),
        cost_estimate=pl.CostEstimate(
            flops=2 * zs * CORES * (owners * SLOTS) * REQ * each * wide,
            bytes_accessed=4 * owners * zs * CORES * SLOTS * wide,
            transcendentals=0,
        ),
    )(blocks, slot_ids, *parts)


def attend_kernel(length, q_ref, k_ref, v_ref, kc_ref, vc_ref, o_ref, *, blocks):
    step = pl.program_id(1)
    size = q_ref.shape[0]
    factor = math.log2(math.e) / math.sqrt(HD)
    contract = (((1,), (1,)), ((), ()))
    slots = kc_ref.shape[0] * kc_ref.shape[1]

    for index in range(blocks):

        @pl.when(step == index)
        def _(index=index):
            query = q_ref[...]
            k_old = kc_ref[...].reshape(slots, HD)
            v_old = vc_ref[...].reshape(slots, HD)
            old = lax.dot_general(query, k_old, contract, preferred_element_type=jnp.float32)
            slot = lax.broadcasted_iota(jnp.int32, old.shape, 1)
            old = jnp.where(slot < length[0], old, MASKED)
            parts = [(old, v_old)]
            if index:
                span = index * size
                parts.append(
                    (
                        lax.dot_general(
                            query, k_ref[:span], contract, preferred_element_type=jnp.float32
                        ),
                        v_ref[:span],
                    )
                )
            own = lax.dot_general(
                query,
                k_ref[index * size : (index + 1) * size],
                contract,
                preferred_element_type=jnp.float32,
            )
            row = lax.broadcasted_iota(jnp.int32, own.shape, 0)
            column = lax.broadcasted_iota(jnp.int32, own.shape, 1)
            own = jnp.where(column <= row, own, MASKED)
            parts.append((own, v_ref[index * size : (index + 1) * size]))
            highest = functools.reduce(
                jnp.maximum, [jnp.max(s, axis=1, keepdims=True) for s, _ in parts]
            )
            total, mixed = 0.0, 0.0
            for scores, values in parts:
                weights = jnp.exp2((scores - highest) * factor)
                total = total + jnp.sum(weights, axis=1, keepdims=True)
                mixed = mixed + jnp.dot(
                    weights.astype(jnp.bfloat16), values, preferred_element_type=jnp.float32
                )
            o_ref[...] = (mixed / total).astype(jnp.bfloat16)


def attend(query, keys, values, cached, length):
    count, width = query.shape
    heads, size = width // HD, min(256, count)
    blocks = count // size
    sources, _, each, _ = cached.shape

    def old(which):
        return pl.BlockSpec((sources, None, each, HD), lambda h, i, s: (0, which, 0, h))

    return pl.pallas_call(
        functools.partial(attend_kernel, blocks=blocks),
        grid_spec=pltpu.PrefetchScalarGridSpec(
            num_scalar_prefetch=1,
            grid=(heads, blocks),
            in_specs=[
                pl.BlockSpec((size, HD), lambda h, i, s: (i, h)),
                pl.BlockSpec((count, HD), lambda h, i, s: (0, h)),
                pl.BlockSpec((count, HD), lambda h, i, s: (0, h)),
                old(0),
                old(1),
            ],
            out_specs=pl.BlockSpec((size, HD), lambda h, i, s: (i, h)),
        ),
        out_shape=jax.ShapeDtypeStruct((count, width), jnp.bfloat16),
        compiler_params=pltpu.CompilerParams(
            vmem_limit_bytes=48 * 2**20, dimension_semantics=("arbitrary", "arbitrary")
        ),
        cost_estimate=pl.CostEstimate(
            flops=4 * count * (count // 2 + sources * each) * width,
            bytes_accessed=2 * 4 * count * width,
            transcendentals=count * (count // 2 + sources * each) * heads,
        ),
    )(jnp.reshape(length, (1,)), query, keys, values, cached, cached)


def output_kernel(place, *refs):
    mine_ref, other_ref, lhs, held, sem_l, sem_w = refs[-6:]
    sources, weights = refs[:CORES], refs[CORES:-6]
    zs = lhs.shape[3] // (sources[0].shape[2] * CORES)
    each, cols = sources[0].shape[1:]
    lanes = weights[0].shape[2]
    depth = lhs.shape[3]
    chip, step = place[0], pl.program_id(0)

    def row_copy(which, z, r, c):
        source = (z * REQ + r) * CORES + c
        return pltpu.make_async_copy(
            sources[which].at[source],
            lhs.at[which, r, :, pl.ds((z * CORES + c) * cols, cols)],
            sem_l.at[which, source],
        )

    row_parts = [
        (which, z, r, c)
        for which in range(CORES)
        for z in range(zs)
        for r in range(REQ)
        for c in range(CORES)
    ]

    def weight_copies(index, r):
        if index == 0:
            pairs = [(weights[0].at[r], held.at[0, :, pl.ds(r * lanes, lanes)])]
        else:
            column = pl.multiple_of((chip ^ r) * lanes, lanes)
            half, first = depth // 2, 5 * index - 4
            pairs = [
                (
                    weights[first + 3 + part].at[0] if r == 3 else weights[first + r].at[part],
                    held.at[index, pl.ds(part * half, half), pl.ds(column, lanes)],
                )
                for part in range(2)
            ]
        return [
            pltpu.make_async_copy(source, target, sem_w.at[index, r, number])
            for number, (source, target) in enumerate(pairs)
        ]

    @pl.when(step == 0)
    def _():
        for part in row_parts:
            row_copy(*part).start()
        for index in range(zs):
            for r in range(REQ):
                for copy in weight_copies(index, r):
                    copy.start()
        for part in row_parts:
            row_copy(*part).wait()

    for index in range(zs):

        @pl.when(step == index)
        def _(index=index):
            for r in range(REQ):
                for copy in weight_copies(index, r):
                    copy.wait()

    rows = lhs[...].reshape(CORES * REQ * each, depth)
    out = jnp.dot(rows, held[step], preferred_element_type=jnp.float32).astype(jnp.bfloat16)
    mine_ref[...] = out[: REQ * each]
    other_ref[...] = out[REQ * each :]


def output(place, back, back_other, weights):
    sources, each, cols = back.shape
    _, depth, lanes = weights[0].shape
    zs = sources // (REQ * CORES)
    anywhere = pl.BlockSpec(memory_space=pl.ANY)
    block = pl.BlockSpec((REQ * each, REQ * lanes), lambda i, s: (0, s[1 + i]))
    shape = jax.ShapeDtypeStruct((REQ * each, zs * REQ * lanes), jnp.bfloat16)
    return pl.pallas_call(
        output_kernel,
        grid_spec=pltpu.PrefetchScalarGridSpec(
            num_scalar_prefetch=1,
            grid=(zs,),
            in_specs=[anywhere] * (CORES + len(weights)),
            out_specs=[block, block],
            scratch_shapes=[
                pltpu.VMEM((CORES, REQ, each, depth), jnp.bfloat16),
                pltpu.VMEM((zs, depth, REQ * lanes), jnp.bfloat16),
                pltpu.SemaphoreType.DMA((CORES, sources)),
                pltpu.SemaphoreType.DMA((zs, REQ, 2)),
            ],
        ),
        out_shape=[shape, shape],
        compiler_params=pltpu.CompilerParams(
            vmem_limit_bytes=56 * 2**20, dimension_semantics=("arbitrary",)
        ),
        cost_estimate=pl.CostEstimate(
            flops=2 * CORES * REQ * each * depth * zs * REQ * lanes,
            bytes_accessed=2 * (2 * back.size + depth * zs * REQ * lanes),
            transcendentals=0,
        ),
    )(place, back, back_other, *weights)


def interleave_kernel(place, mine_ref, other_ref, out_ref):
    lanes = LANES
    core = place[0]
    for block in range(mine_ref.shape[1] // lanes):
        part = slice(block * lanes, (block + 1) * lanes)
        here = pl.multiple_of((CORES * block + core) * lanes, lanes)
        there = pl.multiple_of((CORES * block + 1 - core) * lanes, lanes)
        out_ref[:, pl.ds(here, lanes)] = mine_ref[:, part]
        out_ref[:, pl.ds(there, lanes)] = other_ref[:, part]


def interleave(core, mine, other):
    rows, width = mine.shape
    tile = pl.BlockSpec((rows, width // 2), lambda i, s: (0, i))
    return pl.pallas_call(
        interleave_kernel,
        grid_spec=pltpu.PrefetchScalarGridSpec(
            num_scalar_prefetch=1,
            grid=(2,),
            in_specs=[tile, tile],
            out_specs=pl.BlockSpec((rows, width), lambda i, s: (0, i)),
        ),
        out_shape=jax.ShapeDtypeStruct((rows, CORES * width), mine.dtype),
        compiler_params=pltpu.CompilerParams(dimension_semantics=("arbitrary",)),
        cost_estimate=pl.CostEstimate(
            flops=0, bytes_accessed=8 * rows * width, transcendentals=0
        ),
    )(jnp.reshape(core, (1,)), mine, other)


def slots_of(owners, count):
    marks = (owners[:, None] == jnp.arange(count)[None, :]).astype(jnp.int32)
    earlier = jnp.cumsum(marks, axis=0) - marks
    return owners * SLOTS + jnp.sum(earlier * marks, axis=1)


def swap_chips(value, away):
    return lax.ppermute(value, "r", [(chip, chip ^ away) for chip in range(REQ)])


def swap_cores(value):
    return lax.ppermute(value, "c", [(0, 1), (1, 0)])


def z_step(up, down, step):
    last = Z_CHIPS - 1
    up = lax.ppermute(up, "z", [(z, z + 1) for z in range(step, last)])
    down = lax.ppermute(down, "z", [(z, z - 1) for z in range(1, Z_CHIPS - step)])
    return up, down


def z_last_step(z, up, down):
    out = lax.ppermute(jnp.where(z == 2, up, down), "z", [(2, 3), (1, 0)])
    return out, out


def by_block(z, steps, column):
    up, down = zip(*steps)
    if column == 1:
        return jnp.where(z == 0, down[0], up[0])
    if column == 2:
        return jnp.where(z == 0, down[1], jnp.where(z == 3, up[1], down[0]))
    return jnp.where(
        z == 0, down[2], jnp.where(z == 1, down[1], jnp.where(z == 2, up[1], up[2]))
    )


def block_table():
    return jnp.array([[0, 1, 2, 3], [1, 0, 2, 3], [2, 1, 3, 0], [3, 2, 1, 0]], jnp.int32)


def by_heads(hidden_in, ln_gain, ln_bias, w_qkv, w_out, cache_kv, cache_len, owner):
    zs, seq_count = lax.axis_size("z"), lax.axis_size("z") * REQ * CORES
    groups = zs * CORES
    z, chip, core = lax.axis_index("z"), lax.axis_index("r"), lax.axis_index("c")
    seq = ("z", "r", "c")
    new_dev, depth = hidden_in.shape[1], hidden_in.shape[2]
    width = w_qkv.shape[2]
    cols = width // groups
    blocks = block_table()[z]

    def near(part):
        return part + (swap_chips(part[0], 1), swap_chips(part[0], 2))

    def far(part):
        half = part[1].shape[0] // 2
        return part + (swap_chips(part[1][:half], 2), swap_chips(part[2][half:], 1))

    rows_dev = w_qkv.shape[1]
    w_cut = w_qkv.reshape(3, rows_dev, groups, cols).transpose(2, 0, 1, 3)
    slots_here = slots_of(owner[:, 0], seq_count).astype(jnp.bfloat16)
    slot_rows = jnp.zeros((groups, 8, cols), jnp.bfloat16)
    slot_rows = slot_rows.at[:, 0, : slots_here.shape[0]].set(slots_here[None])
    w_cut = jnp.concatenate([w_cut.reshape(groups, 3 * rows_dev, cols), slot_rows], axis=1)
    w_cut = lax.all_to_all(w_cut, ("z", "c"), split_axis=0, concat_axis=0, tiled=True)

    normed = layer_norm(hidden_in, ln_gain, ln_bias)
    x_own = jnp.stack(
        [
            swap_chips(lax.dynamic_index_in_dim(normed, chip ^ away, 0, keepdims=False), away)
            if away
            else lax.dynamic_index_in_dim(normed, chip, 0, keepdims=False)
            for away in range(REQ)
        ]
    )
    cache_each = cache_kv.shape[1]
    cut = cache_kv.reshape(REQ, cache_each, 2, zs, CORES, cols).transpose(3, 0, 4, 2, 1, 5)
    cut = cut.reshape(seq_count, 2, cache_each, cols)

    length = jnp.sum(jnp.where(jnp.arange(REQ) == chip, cache_len, 0))
    new_len = seq_count * new_dev
    cosine, sine = rotary_tables(length + jnp.arange(new_len))
    shape = (zs, REQ, CORES, new_dev, LANES)
    tables = [table.reshape(shape).transpose(0, 2, 1, 3, 4) for table in (cosine, sine)]

    x_own, w_cut = lax.optimization_barrier((x_own, w_cut))
    w_own = w_cut[:, : 3 * rows_dev].reshape(groups, 3, rows_dev, cols)
    slot_ids = w_cut[:, 3 * rows_dev, : slots_here.shape[0]].astype(jnp.int32)
    slot_ids = slot_ids.reshape(zs, CORES, REQ, new_dev)[blocks]
    near_first = slot_ids[:2, :, chip ^ jnp.arange(REQ)]
    slot_ids = jnp.concatenate([near_first, slot_ids[2:]], axis=0)
    slot_ids = slot_ids.reshape(zs, CORES, 1, REQ * new_dev)

    out_parts = [lax.all_gather(w_out, "r", axis=0, tiled=False)]

    w_parts = [(w_own[:, :2],), (w_own[:, 2:],)]
    x_steps = [z_step(x_own, x_own, 0)]
    other_own = swap_cores(x_own)
    w_parts = [near(w_parts[0]), w_parts[1]]
    x_steps, w_parts, other_own, tables, out_parts = lax.optimization_barrier(
        (x_steps, w_parts, other_own, tables, out_parts)
    )
    x_steps = x_steps + [z_step(*x_steps[0], 1)]
    x_first = by_block(z, x_steps, 1)
    other_first = swap_cores(x_first)
    w_parts = [far(w_parts[0]), near(w_parts[1])]
    x_steps, w_parts, x_first, other_first = lax.optimization_barrier(
        (x_steps, w_parts, x_first, other_first)
    )
    x_steps = x_steps + [z_step(*x_steps[1], 2)]
    x_second = by_block(z, x_steps, 2)
    other_second = swap_cores(x_second)
    w_parts = [w_parts[0], far(w_parts[1])]
    weights = [piece for part in w_parts for piece in part]

    def run(first, pairs, held, cost, by_chip):
        steps = len(pairs) // CORES
        place = jnp.concatenate([jnp.stack([chip, core]), blocks[first : first + steps]])
        place = place.astype(jnp.int32)
        *held, fresh = project(pairs, weights, *tables, place, held, cost, by_chip)
        return held, fresh

    def send(fresh):
        return [fresh[0]] + [swap_chips(fresh[away], away) for away in range(1, REQ)]

    held, fresh = run(0, [x_own, other_own, x_first, other_first], (), 0, False)
    x_steps, held, fresh, x_second, other_second, w_out = lax.optimization_barrier(
        (x_steps, held, fresh, x_second, other_second, w_out)
    )
    out_steps = [z_step(w_out, w_out, 0)]
    x_last = by_block(z, x_steps, 3)
    sent = send(fresh)
    cached = lax.all_to_all(cut, seq, split_axis=0, concat_axis=0, tiled=True)
    pairs = [x_second, other_second, x_last, swap_cores(x_last)]
    held, fresh = run(2, pairs, held, 1, True)
    out_steps, sent, held, fresh, cached = lax.optimization_barrier(
        (out_steps, sent, held, fresh, cached)
    )
    w_first = by_block(z, out_steps, 1)
    w_first = near((w_first.reshape(2, w_first.shape[0] // 2, w_first.shape[1]),))
    out_steps += [z_step(*out_steps[0], 1)]
    whole = lax.all_to_all(fresh, "r", split_axis=0, concat_axis=0, tiled=True)
    sent += [whole[r] for r in range(REQ)]
    query, keys, values = held
    flat = (new_len, cols)

    attended = attend(
        query.reshape(flat), keys.reshape(flat), values.reshape(flat), cached, length
    )
    out_steps, attended, sent, w_first = lax.optimization_barrier(
        (out_steps, attended, sent, w_first)
    )
    out_steps += [z_last_step(z, *out_steps[1])]
    back = lax.all_to_all(
        attended.reshape(seq_count, new_dev, cols), seq, split_axis=0, concat_axis=0, tiled=True
    )
    w_second = by_block(z, out_steps, 2)
    w_second = near((w_second.reshape(2, w_second.shape[0] // 2, w_second.shape[1]),))
    outgoing = order(blocks, slot_ids, sent, seq_count)
    out_parts += far(w_first)
    back, outgoing, out_parts, out_steps, w_second = lax.optimization_barrier(
        (back, outgoing, out_parts, out_steps, w_second)
    )
    out_parts += far(w_second)
    w_third = by_block(z, out_steps, 3)
    out_parts += far(near((w_third.reshape(2, w_third.shape[0] // 2, w_third.shape[1]),)))
    arrived = lax.all_to_all(outgoing, seq, split_axis=0, concat_axis=0, tiled=True)
    appended = arrived.reshape(zs, REQ, CORES, zs, CORES, SLOTS, 2, cols)
    appended = appended.transpose(3, 1, 4, 5, 6, 0, 2, 7).reshape(seq_count * SLOTS, 2, width)

    place = jnp.concatenate([jnp.stack([chip]), blocks]).astype(jnp.int32)
    out, out_other = output(place, back, swap_cores(back), out_parts)
    out = interleave(core, out, swap_cores(out_other))
    return out.reshape(REQ, new_dev, out.shape[1]), appended


def by_tokens(hidden_in, ln_gain, ln_bias, w_qkv, w_out, cache_kv, cache_len, owner):
    new_dev = hidden_in.shape[1]
    tok_rows = REQ * new_dev
    normed = layer_norm(hidden_in.reshape(tok_rows, hidden_in.shape[2]), ln_gain, ln_bias)
    width = w_qkv.shape[2]
    heads_here = width // HD
    seq_count = lax.axis_size("seq")
    seq_here = lax.axis_index("seq")
    cache_each = cache_kv.shape[1]
    cache_dev = REQ * cache_each
    cache_flat = cache_kv.reshape(cache_dev, 2, width)
    rows_dev = cache_dev + tok_rows
    request_ids = jnp.arange(REQ)
    projected = jnp.einsum(
        "tc,icw->itw",
        normed,
        lax.all_gather(w_qkv, "seq", axis=1, tiled=True),
        preferred_element_type=jnp.float32,
    )

    def length_of(requests):
        return jnp.sum(
            jnp.where(requests[:, None] == request_ids[None, :], cache_len[None, :], 0), axis=1
        )

    local_ids = jnp.arange(tok_rows)
    query_req = local_ids // new_dev
    query_pos = length_of(query_req) + seq_here * new_dev + local_ids % new_dev
    shape_heads = (tok_rows, heads_here, HD)
    query = rotate(projected[0].reshape(shape_heads), query_pos).astype(jnp.bfloat16)
    keys_new = (
        rotate(projected[1].reshape(shape_heads), query_pos)
        .astype(jnp.bfloat16)
        .reshape(tok_rows, width)
    )
    values_new = projected[2].astype(jnp.bfloat16)
    fresh = jnp.stack([keys_new, values_new], axis=1)
    local_rows = jnp.concatenate([cache_flat, fresh], axis=0)
    scale_factor = 1.0 / math.sqrt(HD)
    block_rows = lax.all_gather(local_rows, "seq", axis=0, tiled=True)
    count = block_rows.shape[0]
    row_ids = jnp.arange(count)
    source = jnp.floor_divide(row_ids, rows_dev)
    within = row_ids - source * rows_dev
    in_cache = within < cache_dev
    cache_req = jnp.floor_divide(within, cache_each)
    cache_slot = source * cache_each + within - cache_req * cache_each
    new_local = within - cache_dev
    new_req = jnp.floor_divide(new_local, new_dev)
    key_req = jnp.where(in_cache, cache_req, new_req)
    key_len = length_of(key_req)
    key_pos = jnp.where(
        in_cache, cache_slot, key_len + source * new_dev + new_local - new_req * new_dev
    )
    usable = jnp.logical_or(jnp.logical_not(in_cache), cache_slot < key_len)
    allowed = (
        usable[None, :]
        & (key_req[None, :] == query_req[:, None])
        & (key_pos[None, :] <= query_pos[:, None])
    )
    key_rows = block_rows[:, 0].reshape(count, heads_here, HD)
    value_rows = block_rows[:, 1].reshape(count, heads_here, HD)
    scores = (
        jnp.einsum("qhd,khd->hqk", query, key_rows, preferred_element_type=jnp.float32)
        * scale_factor
    )
    scores = jnp.where(allowed[None], scores, MASKED)
    highest = jnp.max(scores, axis=-1)
    weights = jnp.where(allowed[None], jnp.exp(scores - highest[:, :, None]), 0.0)
    weight_sum = jnp.sum(weights, axis=-1)
    weighted = jnp.einsum(
        "hqk,khd->qhd", weights.astype(jnp.bfloat16), value_rows, preferred_element_type=jnp.float32
    )
    attended = (
        (weighted / jnp.transpose(weight_sum)[:, :, None])
        .astype(jnp.bfloat16)
        .reshape(tok_rows, width)
    )
    partial_out = jnp.dot(
        attended,
        lax.all_gather(w_out, "seq", axis=1, tiled=True),
        preferred_element_type=jnp.float32,
    ).astype(jnp.bfloat16)
    summed = (
        lax.psum_scatter(partial_out, "tp", scatter_dimension=1, tiled=True)
        .astype(jnp.float32)
        .astype(jnp.bfloat16)
    )
    attn_out = summed.reshape(REQ, new_dev, summed.shape[1])
    slot_ids = slots_of(owner[:, 0], seq_count)
    placing = (jnp.arange(seq_count * SLOTS)[:, None] == slot_ids[None, :]).astype(jnp.bfloat16)
    outgoing = jnp.einsum("st,tkw->skw", placing, fresh, preferred_element_type=jnp.float32).astype(
        jnp.bfloat16
    )
    outgoing = outgoing.reshape(seq_count, SLOTS, 2, width)
    arrived = lax.all_to_all(outgoing, "seq", split_axis=0, concat_axis=0, tiled=True)
    appended = arrived.reshape(seq_count * SLOTS, 2, width)
    return (attn_out, appended)


def solution(mesh):
    seq_count, tp_count = mesh.shape["seq"], mesh.shape["tp"]
    zs = seq_count // (REQ * CORES)

    def call(*args):
        heads_here = args[3].shape[2] // tp_count // HD
        split = (
            tp_count == 1
            and zs == Z_CHIPS
            and zs * REQ * CORES == seq_count
            and heads_here % max(zs * CORES, 1) == 0
        )
        if split:
            body, seq, names = by_heads, ("z", "r", "c"), ("z", "r", "c", "tp")
            grid = Mesh(mesh.devices.reshape(zs, REQ, CORES, tp_count), names)
        else:
            body, seq, grid = by_tokens, "seq", mesh
        return jax.shard_map(
            body,
            mesh=grid,
            in_specs=(
                P(None, seq, None),
                P(),
                P(),
                P(None, seq, "tp"),
                P("tp", seq),
                P(None, seq, None, "tp"),
                P(),
                P(seq, None),
            ),
            out_specs=(P(None, seq, "tp"), P(seq, None, "tp")),
            check_vma=False,
        )(*args)

    return call
```

```python
import functools
import math

import jax
import jax.numpy as jnp
from jax import lax
from jax.experimental import pallas as pl
from jax.experimental.pallas import tpu as pltpu
from jax.sharding import Mesh
from jax.sharding import PartitionSpec as P

HD = 256
ROT = 64
REQ = 4
SLOTS = 8
CORES = 2
Z_CHIPS = 4

EPSILON = 1e-05
BASE_FREQ = 10000.0
MASKED = -1e30
LANES = 128


def layer_norm(values_in, gain, shift):
    wide = values_in.astype(jnp.float32)
    center = jnp.mean(wide, axis=-1, keepdims=True)
    spread = wide - center
    variance = jnp.mean(spread * spread, axis=-1, keepdims=True)
    return (spread * lax.rsqrt(variance + EPSILON) * gain + shift).astype(jnp.bfloat16)


def rotate(heads_in, positions):
    pair_index = jnp.arange(ROT // 2).astype(jnp.float32)
    inverse = jnp.power(BASE_FREQ, -2.0 * pair_index / ROT)
    angles = positions.astype(jnp.float32)[:, None] * inverse[None, :]
    cosine = jnp.cos(angles)[:, None, :]
    sine = jnp.sin(angles)[:, None, :]
    leading = heads_in.shape[:-1]
    paired = heads_in[..., :ROT].reshape(leading + (ROT // 2, 2))
    even = paired[..., 0]
    odd = paired[..., 1]
    turned = jnp.stack([even * cosine - odd * sine, odd * cosine + even * sine], axis=-1).reshape(
        leading + (ROT,)
    )
    return jnp.concatenate([turned, heads_in[..., ROT:]], axis=-1)


def rotary_tables(positions):
    lane = jnp.arange(LANES)
    pair_index = (lane // 2).astype(jnp.float32)
    inverse = jnp.power(BASE_FREQ, -2.0 * pair_index / ROT)
    angles = positions.astype(jnp.float32)[:, None] * inverse[None, :]
    turned = lane < ROT
    cosine = jnp.where(turned, jnp.cos(angles), 1.0)
    sine = jnp.where(turned, jnp.where(lane % 2 == 0, -1.0, 1.0) * jnp.sin(angles), 0.0)
    return cosine, sine


def project_kernel(place, *refs, by_chip):
    q_ref, k_ref, v_ref, send_ref, rows_ref, held, sem_x, sem_w = refs[-8:]
    steps, _, _, each, depth = rows_ref.shape
    weights, (cos_ref, sin_ref) = refs[:10], refs[10:12]
    sources = refs[12 : 12 + 2 * steps]
    groups, _, rows_each, width = weights[0].shape
    zs = groups // CORES
    chip, core, step = place[0], place[1], pl.program_id(0)

    def row_copy(index, c, away):
        return pltpu.make_async_copy(
            sources[2 * index + c].at[away],
            rows_ref.at[index, core ^ c, chip ^ away],
            sem_x.at[index, c, away],
        )

    def weight_copy(which, away, z, c):
        row = pl.multiple_of(((z * REQ + (chip ^ away)) * CORES + c) * rows_each, rows_each)
        group = z * CORES + c
        piece = away + (away == 3 and group >= groups // 2)
        inside = group - groups // 2 if piece == 4 else group
        return pltpu.make_async_copy(
            weights[5 * (which // 2) + piece].at[inside, which % 2],
            held.at[which, pl.ds(row, rows_each)],
            sem_w.at[which, away, group],
        )

    row_parts = [(c, away) for c in range(CORES) for away in range(REQ)]
    weight_parts = [
        (away, z, c) for away in range(REQ) for z in range(zs) for c in range(CORES)
    ]

    @pl.when(step == 0)
    def _():
        for part in row_parts:
            row_copy(0, *part).start()
        for part in weight_parts:
            weight_copy(0, *part).start()

    for index in range(steps):

        @pl.when(step == index)
        def _(index=index):
            for part in row_parts:
                row_copy(index, *part).wait()

    count = CORES * REQ * each
    lane = lax.broadcasted_iota(jnp.int32, (count, LANES), 1)
    even = lane % 2 == 0
    cosine = cos_ref[...].reshape(count, LANES)
    sine = sin_ref[...].reshape(count, LANES)
    for which in range(3):

        @pl.when(step == 0)
        def _(which=which):
            for part in weight_parts:
                weight_copy(which, *part).wait()
            if which < 2:
                for part in weight_parts:
                    weight_copy(which + 1, *part).start()
            else:
                for index in range(1, steps):
                    for part in row_parts:
                        row_copy(index, *part).start()

        rows = rows_ref[step].reshape(count, depth)
        out = jnp.dot(rows, held[which], preferred_element_type=jnp.float32)
        if which < 2:
            pieces = []
            for head in range(width // HD):
                low = out[:, head * HD : head * HD + LANES]
                other = jnp.where(even, pltpu.roll(low, LANES - 1, 1), pltpu.roll(low, 1, 1))
                pieces.append(low * cosine + other * sine)
                pieces.append(out[:, head * HD + LANES : (head + 1) * HD])
            out = jnp.concatenate(pieces, axis=1)
        out = out.astype(jnp.bfloat16).reshape(CORES, REQ, each, width)
        for c in range(CORES):
            for r in range(REQ):
                part = out[c, r]
                if which == 0:
                    q_ref[0, r, c] = part
                elif which == 1:
                    k_ref[0, r, c] = part
                    send_ref[r if by_chip else r ^ chip, 0, c, :, :width] = part
                else:
                    v_ref[0, r, c] = part
                    send_ref[r if by_chip else r ^ chip, 0, c, :, width:] = part


def project(x_pairs, weights, cosine, sine, place, held, cost, by_chip):
    steps = len(x_pairs) // CORES
    _, each, depth = x_pairs[0].shape
    groups, _, rows_each, width = weights[0].shape
    zs = groups // CORES
    table = pl.BlockSpec((1, CORES, REQ, each, LANES), lambda i, s: (s[2 + i], 0, 0, 0, 0))
    token = pl.BlockSpec((1, REQ, CORES, each, width), lambda i, s: (s[2 + i], 0, 0, 0, 0))
    whole = jax.ShapeDtypeStruct((zs, REQ, CORES, each, width), jnp.bfloat16)
    anywhere = pl.BlockSpec(memory_space=pl.ANY)
    return pl.pallas_call(
        functools.partial(project_kernel, by_chip=by_chip),
        grid_spec=pltpu.PrefetchScalarGridSpec(
            num_scalar_prefetch=1,
            grid=(steps,),
            in_specs=[anywhere] * len(weights)
            + [table, table]
            + [anywhere] * (len(x_pairs) + len(held)),
            out_specs=[
                token,
                token,
                token,
                pl.BlockSpec(
                    (REQ, 1, CORES, each, 2 * width), lambda i, s: (0, i, 0, 0, 0)
                ),
            ],
            scratch_shapes=[
                pltpu.VMEM((steps, CORES, REQ, each, depth), jnp.bfloat16),
                pltpu.VMEM((3, depth, width), jnp.bfloat16),
                pltpu.SemaphoreType.DMA((steps, CORES, REQ)),
                pltpu.SemaphoreType.DMA((3, REQ, groups)),
            ],
        ),
        out_shape=[
            whole,
            whole,
            whole,
            jax.ShapeDtypeStruct((REQ, steps, CORES, each, 2 * width), jnp.bfloat16),
        ],
        input_output_aliases={3 + len(weights) + len(x_pairs) + i: i for i in range(len(held))},
        compiler_params=pltpu.CompilerParams(
            vmem_limit_bytes=58 * 2**20, dimension_semantics=("arbitrary",)
        ),
        cost_estimate=pl.CostEstimate(
            flops=2 * steps * CORES * REQ * each * depth * 3 * width * cost,
            bytes_accessed=2 * (x_pairs[0].size * len(x_pairs) + 3 * depth * width) * cost,
            transcendentals=0,
        ),
    )(place, *weights, cosine, sine, *x_pairs, *held)


def order_kernel(blocks, slot_ref, *refs):
    out_ref = refs[-1]
    owners = out_ref.shape[0]
    count = slot_ref.shape[3]
    wanted = lax.broadcasted_iota(jnp.int32, (owners * SLOTS, count), 0)
    index = 0
    for call in range(len(refs) // REQ):
        parts = refs[call * REQ : (call + 1) * REQ]
        for step in range(parts[0].shape[0]):
            ordered = []
            for c in range(CORES):
                placing = (wanted == slot_ref[index, c]).astype(jnp.bfloat16)
                rows = jnp.concatenate([part[step, c] for part in parts], axis=0)
                out = jnp.dot(placing, rows, preferred_element_type=jnp.float32)
                ordered.append(out.reshape(owners, SLOTS, rows.shape[1]))
            both = jnp.concatenate(ordered, axis=1).astype(jnp.bfloat16)
            out_ref[:, pl.ds(blocks[index], 1)] = both[:, None]
            index += 1


def order(blocks, slot_ids, parts, owners):
    zs = slot_ids.shape[0]
    each, wide = parts[0].shape[-2:]
    out = (owners, zs, CORES * SLOTS, wide)
    return pl.pallas_call(
        order_kernel,
        grid_spec=pltpu.PrefetchScalarGridSpec(
            num_scalar_prefetch=1,
            grid=(1,),
            in_specs=[pl.BlockSpec(slot_ids.shape, lambda i, s: (0, 0, 0, 0))]
            + [pl.BlockSpec(part.shape, lambda i, s: (0, 0, 0, 0)) for part in parts],
            out_specs=pl.BlockSpec(out, lambda i, s: (0, 0, 0, 0)),
        ),
        out_shape=jax.ShapeDtypeStruct(out, jnp.bfloat16),
        compiler_params=pltpu.CompilerParams(
            vmem_limit_bytes=56 * 2**20, dimension_semantics=("arbitrary",)
        ),
        cost_estimate=pl.CostEstimate(
            flops=2 * zs * CORES * (owners * SLOTS) * REQ * each * wide,
            bytes_accessed=4 * owners * zs * CORES * SLOTS * wide,
            transcendentals=0,
        ),
    )(blocks, slot_ids, *parts)


def attend_kernel(length, q_ref, k_ref, v_ref, kc_ref, vc_ref, o_ref, *, blocks):
    step = pl.program_id(1)
    size = q_ref.shape[0]
    factor = math.log2(math.e) / math.sqrt(HD)
    contract = (((1,), (1,)), ((), ()))
    slots = kc_ref.shape[0] * kc_ref.shape[1]

    for index in range(blocks):

        @pl.when(step == index)
        def _(index=index):
            query = q_ref[...]
            k_old = kc_ref[...].reshape(slots, HD)
            v_old = vc_ref[...].reshape(slots, HD)
            old = lax.dot_general(query, k_old, contract, preferred_element_type=jnp.float32)
            slot = lax.broadcasted_iota(jnp.int32, old.shape, 1)
            old = jnp.where(slot < length[0], old, MASKED)
            parts = [(old, v_old)]
            if index:
                span = index * size
                parts.append(
                    (
                        lax.dot_general(
                            query, k_ref[:span], contract, preferred_element_type=jnp.float32
                        ),
                        v_ref[:span],
                    )
                )
            own = lax.dot_general(
                query,
                k_ref[index * size : (index + 1) * size],
                contract,
                preferred_element_type=jnp.float32,
            )
            row = lax.broadcasted_iota(jnp.int32, own.shape, 0)
            column = lax.broadcasted_iota(jnp.int32, own.shape, 1)
            own = jnp.where(column <= row, own, MASKED)
            parts.append((own, v_ref[index * size : (index + 1) * size]))
            highest = functools.reduce(
                jnp.maximum, [jnp.max(s, axis=1, keepdims=True) for s, _ in parts]
            )
            total, mixed = 0.0, 0.0
            for scores, values in parts:
                weights = jnp.exp2((scores - highest) * factor)
                total = total + jnp.sum(weights, axis=1, keepdims=True)
                mixed = mixed + jnp.dot(
                    weights.astype(jnp.bfloat16), values, preferred_element_type=jnp.float32
                )
            o_ref[...] = (mixed / total).astype(jnp.bfloat16)


def attend(query, keys, values, cached, length):
    count, width = query.shape
    heads, size = width // HD, min(256, count)
    blocks = count // size
    sources, _, each, _ = cached.shape

    def old(which):
        return pl.BlockSpec((sources, None, each, HD), lambda h, i, s: (0, which, 0, h))

    return pl.pallas_call(
        functools.partial(attend_kernel, blocks=blocks),
        grid_spec=pltpu.PrefetchScalarGridSpec(
            num_scalar_prefetch=1,
            grid=(heads, blocks),
            in_specs=[
                pl.BlockSpec((size, HD), lambda h, i, s: (i, h)),
                pl.BlockSpec((count, HD), lambda h, i, s: (0, h)),
                pl.BlockSpec((count, HD), lambda h, i, s: (0, h)),
                old(0),
                old(1),
            ],
            out_specs=pl.BlockSpec((size, HD), lambda h, i, s: (i, h)),
        ),
        out_shape=jax.ShapeDtypeStruct((count, width), jnp.bfloat16),
        compiler_params=pltpu.CompilerParams(
            vmem_limit_bytes=48 * 2**20, dimension_semantics=("arbitrary", "arbitrary")
        ),
        cost_estimate=pl.CostEstimate(
            flops=4 * count * (count // 2 + sources * each) * width,
            bytes_accessed=2 * 4 * count * width,
            transcendentals=count * (count // 2 + sources * each) * heads,
        ),
    )(jnp.reshape(length, (1,)), query, keys, values, cached, cached)


def output_kernel(place, *refs, pieces, whole):
    mine_ref, other_ref, lhs, held, sem_l, sem_w = refs[-6:]
    sources, weights = refs[:CORES], refs[CORES : CORES + pieces]
    steps = held.shape[0]
    zs = lhs.shape[3] // (sources[0].shape[2] * CORES)
    each, cols = sources[0].shape[1:]
    lanes = weights[0].shape[2]
    depth = lhs.shape[3]
    chip, step = place[0], pl.program_id(0)

    def row_copy(which, z, r, c):
        source = (z * REQ + r) * CORES + c
        return pltpu.make_async_copy(
            sources[which].at[source],
            lhs.at[which, r, :, pl.ds((z * CORES + c) * cols, cols)],
            sem_l.at[which, source],
        )

    row_parts = [
        (which, z, r, c)
        for which in range(CORES)
        for z in range(zs)
        for r in range(REQ)
        for c in range(CORES)
    ]

    def weight_copies(index, r):
        if index < whole:
            pairs = [(weights[index].at[r], held.at[index, :, pl.ds(r * lanes, lanes)])]
        else:
            column = pl.multiple_of((chip ^ r) * lanes, lanes)
            half, first = depth // 2, 5 * index - 4 * whole
            pairs = [
                (
                    weights[first + 3 + part].at[0] if r == 3 else weights[first + r].at[part],
                    held.at[index, pl.ds(part * half, half), pl.ds(column, lanes)],
                )
                for part in range(2)
            ]
        return [
            pltpu.make_async_copy(source, target, sem_w.at[index, r, number])
            for number, (source, target) in enumerate(pairs)
        ]

    @pl.when(step == 0)
    def _():
        for part in row_parts:
            row_copy(*part).start()
        for index in range(steps):
            for r in range(REQ):
                for copy in weight_copies(index, r):
                    copy.start()
        for part in row_parts:
            row_copy(*part).wait()

    for index in range(steps):

        @pl.when(step == index)
        def _(index=index):
            for r in range(REQ):
                for copy in weight_copies(index, r):
                    copy.wait()

    rows = lhs[...].reshape(CORES * REQ * each, depth)
    out = jnp.dot(rows, held[step], preferred_element_type=jnp.float32).astype(jnp.bfloat16)
    mine_ref[...] = out[: REQ * each]
    other_ref[...] = out[REQ * each :]


def output(place, back, back_other, weights, whole, held):
    sources, each, cols = back.shape
    lanes, depth = weights[0].shape[2], sources // REQ * cols
    zs = sources // (REQ * CORES)
    steps = whole + (len(weights) - whole) // 5
    anywhere = pl.BlockSpec(memory_space=pl.ANY)
    block = pl.BlockSpec((REQ * each, REQ * lanes), lambda i, s: (0, s[1 + i]))
    shape = jax.ShapeDtypeStruct((REQ * each, zs * REQ * lanes), jnp.bfloat16)
    return pl.pallas_call(
        functools.partial(output_kernel, pieces=len(weights), whole=whole),
        grid_spec=pltpu.PrefetchScalarGridSpec(
            num_scalar_prefetch=1,
            grid=(steps,),
            in_specs=[anywhere] * (CORES + len(weights) + len(held)),
            out_specs=[block, block],
            scratch_shapes=[
                pltpu.VMEM((CORES, REQ, each, depth), jnp.bfloat16),
                pltpu.VMEM((steps, depth, REQ * lanes), jnp.bfloat16),
                pltpu.SemaphoreType.DMA((CORES, sources)),
                pltpu.SemaphoreType.DMA((steps, REQ, 2)),
            ],
        ),
        out_shape=[shape, shape],
        input_output_aliases={1 + CORES + len(weights) + i: i for i in range(len(held))},
        compiler_params=pltpu.CompilerParams(
            vmem_limit_bytes=56 * 2**20, dimension_semantics=("arbitrary",)
        ),
        cost_estimate=pl.CostEstimate(
            flops=2 * CORES * REQ * each * depth * steps * REQ * lanes,
            bytes_accessed=2 * (2 * back.size + depth * steps * REQ * lanes),
            transcendentals=0,
        ),
    )(place, back, back_other, *weights, *held)


def interleave_kernel(place, mine_ref, other_ref, out_ref):
    lanes = LANES
    core = place[0]
    for block in range(mine_ref.shape[1] // lanes):
        part = slice(block * lanes, (block + 1) * lanes)
        here = pl.multiple_of((CORES * block + core) * lanes, lanes)
        there = pl.multiple_of((CORES * block + 1 - core) * lanes, lanes)
        out_ref[:, pl.ds(here, lanes)] = mine_ref[:, part]
        out_ref[:, pl.ds(there, lanes)] = other_ref[:, part]


def interleave(core, mine, other):
    rows, width = mine.shape
    tile = pl.BlockSpec((rows, width // 2), lambda i, s: (0, i))
    return pl.pallas_call(
        interleave_kernel,
        grid_spec=pltpu.PrefetchScalarGridSpec(
            num_scalar_prefetch=1,
            grid=(2,),
            in_specs=[tile, tile],
            out_specs=pl.BlockSpec((rows, width), lambda i, s: (0, i)),
        ),
        out_shape=jax.ShapeDtypeStruct((rows, CORES * width), mine.dtype),
        compiler_params=pltpu.CompilerParams(dimension_semantics=("arbitrary",)),
        cost_estimate=pl.CostEstimate(
            flops=0, bytes_accessed=8 * rows * width, transcendentals=0
        ),
    )(jnp.reshape(core, (1,)), mine, other)


def slots_of(owners, count):
    marks = (owners[:, None] == jnp.arange(count)[None, :]).astype(jnp.int32)
    earlier = jnp.cumsum(marks, axis=0) - marks
    return owners * SLOTS + jnp.sum(earlier * marks, axis=1)


def swap_chips(value, away):
    return lax.ppermute(value, "r", [(chip, chip ^ away) for chip in range(REQ)])


def swap_cores(value):
    return lax.ppermute(value, "c", [(0, 1), (1, 0)])


def z_step(up, down, step):
    last = Z_CHIPS - 1
    up = lax.ppermute(up, "z", [(z, z + 1) for z in range(step, last)])
    down = lax.ppermute(down, "z", [(z, z - 1) for z in range(1, Z_CHIPS - step)])
    return up, down


def z_last_step(z, up, down):
    out = lax.ppermute(jnp.where(z == 2, up, down), "z", [(2, 3), (1, 0)])
    return out, out


def by_block(z, steps, column):
    up, down = zip(*steps)
    if column == 1:
        return jnp.where(z == 0, down[0], up[0])
    if column == 2:
        return jnp.where(z == 0, down[1], jnp.where(z == 3, up[1], down[0]))
    return jnp.where(
        z == 0, down[2], jnp.where(z == 1, down[1], jnp.where(z == 2, up[1], up[2]))
    )


def block_table():
    return jnp.array([[0, 1, 2, 3], [1, 0, 2, 3], [2, 1, 3, 0], [3, 2, 1, 0]], jnp.int32)


def by_heads(hidden_in, ln_gain, ln_bias, w_qkv, w_out, cache_kv, cache_len, owner):
    zs, seq_count = lax.axis_size("z"), lax.axis_size("z") * REQ * CORES
    groups = zs * CORES
    z, chip, core = lax.axis_index("z"), lax.axis_index("r"), lax.axis_index("c")
    seq = ("z", "r", "c")
    new_dev, depth = hidden_in.shape[1], hidden_in.shape[2]
    width = w_qkv.shape[2]
    cols = width // groups
    blocks = block_table()[z]

    def near(part):
        return part + (swap_chips(part[0], 1), swap_chips(part[0], 2))

    def far(part):
        half = part[1].shape[0] // 2
        return part + (swap_chips(part[1][:half], 2), swap_chips(part[2][half:], 1))

    rows_dev = w_qkv.shape[1]
    w_cut = w_qkv.reshape(3, rows_dev, groups, cols).transpose(2, 0, 1, 3)
    slots_here = slots_of(owner[:, 0], seq_count).astype(jnp.bfloat16)
    slot_rows = jnp.zeros((groups, 8, cols), jnp.bfloat16)
    slot_rows = slot_rows.at[:, 0, : slots_here.shape[0]].set(slots_here[None])
    w_cut = jnp.concatenate([w_cut.reshape(groups, 3 * rows_dev, cols), slot_rows], axis=1)
    w_cut = lax.all_to_all(w_cut, ("z", "c"), split_axis=0, concat_axis=0, tiled=True)

    normed = layer_norm(hidden_in, ln_gain, ln_bias)
    x_own = jnp.stack(
        [
            swap_chips(lax.dynamic_index_in_dim(normed, chip ^ away, 0, keepdims=False), away)
            if away
            else lax.dynamic_index_in_dim(normed, chip, 0, keepdims=False)
            for away in range(REQ)
        ]
    )
    cache_each = cache_kv.shape[1]
    cut = cache_kv.reshape(REQ, cache_each, 2, zs, CORES, cols).transpose(3, 0, 4, 2, 1, 5)
    cut = cut.reshape(seq_count, 2, cache_each, cols)

    length = jnp.sum(jnp.where(jnp.arange(REQ) == chip, cache_len, 0))
    new_len = seq_count * new_dev
    cosine, sine = rotary_tables(length + jnp.arange(new_len))
    shape = (zs, REQ, CORES, new_dev, LANES)
    tables = [table.reshape(shape).transpose(0, 2, 1, 3, 4) for table in (cosine, sine)]

    x_own, w_cut = lax.optimization_barrier((x_own, w_cut))
    w_own = w_cut[:, : 3 * rows_dev].reshape(groups, 3, rows_dev, cols)
    slot_ids = w_cut[:, 3 * rows_dev, : slots_here.shape[0]].astype(jnp.int32)
    slot_ids = slot_ids.reshape(zs, CORES, REQ, new_dev)[blocks]
    near_first = slot_ids[:2, :, chip ^ jnp.arange(REQ)]
    slot_ids = jnp.concatenate([near_first, slot_ids[2:]], axis=0)
    slot_ids = slot_ids.reshape(zs, CORES, 1, REQ * new_dev)

    out_parts = [lax.all_gather(w_out, "r", axis=0, tiled=False)]

    w_parts = [(w_own[:, :2],), (w_own[:, 2:],)]
    x_steps = [z_step(x_own, x_own, 0)]
    other_own = swap_cores(x_own)
    w_parts = [near(w_parts[0]), w_parts[1]]
    x_steps, w_parts, other_own, tables, out_parts = lax.optimization_barrier(
        (x_steps, w_parts, other_own, tables, out_parts)
    )
    x_steps = x_steps + [z_step(*x_steps[0], 1)]
    x_first = by_block(z, x_steps, 1)
    other_first = swap_cores(x_first)
    w_parts = [far(w_parts[0]), near(w_parts[1])]
    x_steps, w_parts, x_first, other_first = lax.optimization_barrier(
        (x_steps, w_parts, x_first, other_first)
    )
    x_steps = x_steps + [z_step(*x_steps[1], 2)]
    x_second = by_block(z, x_steps, 2)
    other_second = swap_cores(x_second)
    w_parts = [w_parts[0], far(w_parts[1])]
    weights = [piece for part in w_parts for piece in part]

    def run(first, pairs, held, cost, by_chip):
        steps = len(pairs) // CORES
        place = jnp.concatenate([jnp.stack([chip, core]), blocks[first : first + steps]])
        place = place.astype(jnp.int32)
        *held, fresh = project(pairs, weights, *tables, place, held, cost, by_chip)
        return held, fresh

    def send(fresh):
        return [fresh[0]] + [swap_chips(fresh[away], away) for away in range(1, REQ)]

    held, fresh = run(0, [x_own, other_own, x_first, other_first], (), 0, False)
    x_steps, held, fresh, x_second, other_second, w_out = lax.optimization_barrier(
        (x_steps, held, fresh, x_second, other_second, w_out)
    )
    out_steps = [z_step(w_out, w_out, 0)]
    x_last = by_block(z, x_steps, 3)
    sent = send(fresh)
    cached = lax.all_to_all(cut, seq, split_axis=0, concat_axis=0, tiled=True)
    pairs = [x_second, other_second, x_last, swap_cores(x_last)]
    held, fresh = run(2, pairs, held, 1, True)
    out_steps, sent, held, fresh, cached = lax.optimization_barrier(
        (out_steps, sent, held, fresh, cached)
    )
    w_first = by_block(z, out_steps, 1)
    w_first = near((w_first.reshape(2, w_first.shape[0] // 2, w_first.shape[1]),))
    out_steps += [z_step(*out_steps[0], 1)]
    whole = lax.all_to_all(fresh, "r", split_axis=0, concat_axis=0, tiled=True)
    sent += [whole[r] for r in range(REQ)]
    query, keys, values = held
    flat = (new_len, cols)

    attended = attend(
        query.reshape(flat), keys.reshape(flat), values.reshape(flat), cached, length
    )
    out_steps, attended, sent, w_first = lax.optimization_barrier(
        (out_steps, attended, sent, w_first)
    )
    out_steps += [z_last_step(z, *out_steps[1])]
    back = lax.all_to_all(
        attended.reshape(seq_count, new_dev, cols), seq, split_axis=0, concat_axis=0, tiled=True
    )
    w_second = by_block(z, out_steps, 2)
    w_second = near((w_second.reshape(2, w_second.shape[0] // 2, w_second.shape[1]),))
    outgoing = order(blocks, slot_ids, sent, seq_count)
    out_parts += far(w_first)
    back, outgoing, out_parts, out_steps, w_second = lax.optimization_barrier(
        (back, outgoing, out_parts, out_steps, w_second)
    )
    out_parts += far(w_second)
    w_third = by_block(z, out_steps, 3)
    out_parts += far(near((w_third.reshape(2, w_third.shape[0] // 2, w_third.shape[1]),)))
    arrived = lax.all_to_all(outgoing, seq, split_axis=0, concat_axis=0, tiled=True)
    appended = arrived.reshape(zs, REQ, CORES, zs, CORES, SLOTS, 2, cols)
    appended = appended.transpose(3, 1, 4, 5, 6, 0, 2, 7).reshape(seq_count * SLOTS, 2, width)

    place = jnp.concatenate([jnp.stack([chip]), blocks]).astype(jnp.int32)
    back_other = swap_cores(back)
    outs = output(place[: zs], back, back_other, out_parts[:-5], 1, ())
    last = jnp.concatenate([place[:1], place[zs:]])
    out, out_other = output(last, back, back_other, out_parts[-5:], 0, outs)
    out = interleave(core, out, swap_cores(out_other))
    return out.reshape(REQ, new_dev, out.shape[1]), appended


def by_tokens(hidden_in, ln_gain, ln_bias, w_qkv, w_out, cache_kv, cache_len, owner):
    new_dev = hidden_in.shape[1]
    tok_rows = REQ * new_dev
    normed = layer_norm(hidden_in.reshape(tok_rows, hidden_in.shape[2]), ln_gain, ln_bias)
    width = w_qkv.shape[2]
    heads_here = width // HD
    seq_count = lax.axis_size("seq")
    seq_here = lax.axis_index("seq")
    cache_each = cache_kv.shape[1]
    cache_dev = REQ * cache_each
    cache_flat = cache_kv.reshape(cache_dev, 2, width)
    rows_dev = cache_dev + tok_rows
    request_ids = jnp.arange(REQ)
    projected = jnp.einsum(
        "tc,icw->itw",
        normed,
        lax.all_gather(w_qkv, "seq", axis=1, tiled=True),
        preferred_element_type=jnp.float32,
    )

    def length_of(requests):
        return jnp.sum(
            jnp.where(requests[:, None] == request_ids[None, :], cache_len[None, :], 0), axis=1
        )

    local_ids = jnp.arange(tok_rows)
    query_req = local_ids // new_dev
    query_pos = length_of(query_req) + seq_here * new_dev + local_ids % new_dev
    shape_heads = (tok_rows, heads_here, HD)
    query = rotate(projected[0].reshape(shape_heads), query_pos).astype(jnp.bfloat16)
    keys_new = (
        rotate(projected[1].reshape(shape_heads), query_pos)
        .astype(jnp.bfloat16)
        .reshape(tok_rows, width)
    )
    values_new = projected[2].astype(jnp.bfloat16)
    fresh = jnp.stack([keys_new, values_new], axis=1)
    local_rows = jnp.concatenate([cache_flat, fresh], axis=0)
    scale_factor = 1.0 / math.sqrt(HD)
    block_rows = lax.all_gather(local_rows, "seq", axis=0, tiled=True)
    count = block_rows.shape[0]
    row_ids = jnp.arange(count)
    source = jnp.floor_divide(row_ids, rows_dev)
    within = row_ids - source * rows_dev
    in_cache = within < cache_dev
    cache_req = jnp.floor_divide(within, cache_each)
    cache_slot = source * cache_each + within - cache_req * cache_each
    new_local = within - cache_dev
    new_req = jnp.floor_divide(new_local, new_dev)
    key_req = jnp.where(in_cache, cache_req, new_req)
    key_len = length_of(key_req)
    key_pos = jnp.where(
        in_cache, cache_slot, key_len + source * new_dev + new_local - new_req * new_dev
    )
    usable = jnp.logical_or(jnp.logical_not(in_cache), cache_slot < key_len)
    allowed = (
        usable[None, :]
        & (key_req[None, :] == query_req[:, None])
        & (key_pos[None, :] <= query_pos[:, None])
    )
    key_rows = block_rows[:, 0].reshape(count, heads_here, HD)
    value_rows = block_rows[:, 1].reshape(count, heads_here, HD)
    scores = (
        jnp.einsum("qhd,khd->hqk", query, key_rows, preferred_element_type=jnp.float32)
        * scale_factor
    )
    scores = jnp.where(allowed[None], scores, MASKED)
    highest = jnp.max(scores, axis=-1)
    weights = jnp.where(allowed[None], jnp.exp(scores - highest[:, :, None]), 0.0)
    weight_sum = jnp.sum(weights, axis=-1)
    weighted = jnp.einsum(
        "hqk,khd->qhd", weights.astype(jnp.bfloat16), value_rows, preferred_element_type=jnp.float32
    )
    attended = (
        (weighted / jnp.transpose(weight_sum)[:, :, None])
        .astype(jnp.bfloat16)
        .reshape(tok_rows, width)
    )
    partial_out = jnp.dot(
        attended,
        lax.all_gather(w_out, "seq", axis=1, tiled=True),
        preferred_element_type=jnp.float32,
    ).astype(jnp.bfloat16)
    summed = (
        lax.psum_scatter(partial_out, "tp", scatter_dimension=1, tiled=True)
        .astype(jnp.float32)
        .astype(jnp.bfloat16)
    )
    attn_out = summed.reshape(REQ, new_dev, summed.shape[1])
    slot_ids = slots_of(owner[:, 0], seq_count)
    placing = (jnp.arange(seq_count * SLOTS)[:, None] == slot_ids[None, :]).astype(jnp.bfloat16)
    outgoing = jnp.einsum("st,tkw->skw", placing, fresh, preferred_element_type=jnp.float32).astype(
        jnp.bfloat16
    )
    outgoing = outgoing.reshape(seq_count, SLOTS, 2, width)
    arrived = lax.all_to_all(outgoing, "seq", split_axis=0, concat_axis=0, tiled=True)
    appended = arrived.reshape(seq_count * SLOTS, 2, width)
    return (attn_out, appended)


def solution(mesh):
    seq_count, tp_count = mesh.shape["seq"], mesh.shape["tp"]
    zs = seq_count // (REQ * CORES)

    def call(*args):
        heads_here = args[3].shape[2] // tp_count // HD
        split = (
            tp_count == 1
            and zs == Z_CHIPS
            and zs * REQ * CORES == seq_count
            and heads_here % max(zs * CORES, 1) == 0
        )
        if split:
            body, seq, names = by_heads, ("z", "r", "c"), ("z", "r", "c", "tp")
            grid = Mesh(mesh.devices.reshape(zs, REQ, CORES, tp_count), names)
        else:
            body, seq, grid = by_tokens, "seq", mesh
        return jax.shard_map(
            body,
            mesh=grid,
            in_specs=(
                P(None, seq, None),
                P(),
                P(),
                P(None, seq, "tp"),
                P("tp", seq),
                P(None, seq, None, "tp"),
                P(),
                P(seq, None),
            ),
            out_specs=(P(None, seq, "tp"), P(seq, None, "tp")),
            check_vma=False,
        )(*args)

    return call
```
